256 devices in a mesh: section: 8 (over z), expert: 8 (over x, y_hi), dp: 4 (over y_lo, core).
Axes of the slice: x: 4, y: 4 (y_hi: 2, y_lo: 2; y = y_hi * 2 + y_lo), z: 8, core: 2. Of those that a mesh axis runs over, the one named last changes fastest.
Arguments:
- hidden: bfloat16 [8, 4096, 1024], P('section', ('expert', 'dp')), may hold values from -6 to 6
- expert_ids: int32 [8, 4096, 2], P('section', ('expert', 'dp')), may hold values from 0 to 7, all different within a row; in each aligned block of 128 rows (0 to 127, 128 to 255, ..., all dimensions but the last counted through in order) at most 48 rows name the same one
- cotangent: bfloat16 [8, 4096, 1024], P('section', ('expert', 'dp')), may hold values from -6 to 6
- skip_weight: bfloat16 [8, 2048, 1024], P('section'), may hold values from -0.125 to 0.125
- norm_gain: float32 [8, 1024], P('section'), may hold values from 0.25 to 1.75
- router_weight: bfloat16 [8, 1024, 8], P('section'), may hold values from -0.1875 to 0.1875
- gate_weight: bfloat16 [8, 8, 1024, 1024], P('section', 'expert'), may hold values from -0.1875 to 0.1875
- up_weight: bfloat16 [8, 8, 1024, 1024], P('section', 'expert'), may hold values from -0.1875 to 0.1875
- down_weight: bfloat16 [8, 8, 1024, 1024], P('section', 'expert'), may hold values from -0.1875 to 0.1875
Outputs:
- section_out: bfloat16 [8, 4096, 1024], P('section', ('expert', 'dp'))
- hidden_grad: bfloat16 [8, 4096, 1024], P('section', ('expert', 'dp'))
- skip_grad: float32 [8, 2048, 1024], P('section', ('expert', 'dp'))
- router_grad: float32 [8, 1024, 8], P('section')
- gain_grad: float32 [8, 1024], P('section')
The draws below stay inside these ranges and needn't reach their ends.
Inputs may be any that keep to these rules, and one draw needn't show every extreme that they name: `expert_ids`: in the rows of one device (aligned blocks of 128 frames of each section) no expert is named more than 48 times; the two experts of a frame differ.
All inputs are finite; a program needn't handle non-finite values.
Results may differ from the reference program's by a relative error of at most 0.029.
Values may be sent and summed in bfloat16 or wider, within the bound.
A program may use at most 128 MiB of HBM per device.

```python
import math
import jax
import jax.numpy as jnp
import numpy as np
from jax import lax

D = 1024
FF = 1024
TOK_DEV = 128
SECTIONS = 8
EXPERTS = 8
CAP = 48
TOKENS = 4096
N_EXPERT = 8
N_DP = 4


def spiked(entries, key, source, target, shards_of, factor):
    def block_of(axis_at):
        return (jnp.arange(entries.shape[axis_at]) // (entries.shape[axis_at] // shards_of)).reshape((-1,) + (1,) * (entries.ndim - 1 - axis_at))

    first = jax.random.permutation(key, shards_of)[block_of(target)]
    second = (block_of(target) + shards_of // 2) % shards_of
    return jnp.where((block_of(source) == first) | (block_of(source) == second), factor * entries, entries)


def block_scale(stream_key, dims, pieces, low, high):
    gain, own = 1.0, jax.random.fold_in(stream_key, 6)
    for position, blocks in pieces:
        heights = jnp.exp(jax.random.uniform(jax.random.fold_in(own, position), (blocks,), jnp.float32, low / len(pieces), high / len(pieces)))
        gain = gain * jnp.repeat(heights, dims[position] // blocks).reshape([-1 if axis == position else 1 for axis in range(len(dims))])
    return gain


def deal_out(stream_key, own, number, rows, number_of, top, bound, lean):
    sequence = jax.random.permutation(stream_key, number_of)
    heavy_load, usual = portions_of(number_of, rows * top, bound, lean, True), portions_of(number_of, rows * top, bound, lean, False)
    places = jnp.arange(number_of)

    def named(lengths, rotation):
        used = int((lengths > 0).sum())
        fixed = max(1, used // 4)
        shifted = fixed + (places - fixed + rotation * (used - fixed)) % max(1, number_of - fixed)
        return jnp.zeros((number_of,), jnp.int32).at[sequence[jnp.where(places < fixed, places, shifted)]].set(jnp.asarray(lengths, jnp.int32))

    lengths = jnp.where(number % 4 == 0, named(heavy_load, number // 4), named(usual, number - number // 4 - 1))
    mixed = jax.random.permutation(jax.random.fold_in(own, 3), number_of)
    source_of, sink = mixed[0:number_of // 2 * 2:2], mixed[1:number_of // 2 * 2:2]
    margin = jnp.minimum(lengths[source_of] - 1, bound - lengths[sink]) // 2
    margin = jnp.where((source_of == sequence[0]) | (sink == sequence[0]) | (lengths[sink] == 0), 0, jnp.maximum(margin, 0))
    shifted = jax.random.randint(jax.random.fold_in(own, 4), (number_of // 2,), 0, 1 << 20) % (margin + 1)
    lengths = lengths.at[source_of].add(-shifted).at[sink].add(shifted)
    members = jnp.searchsorted(jnp.cumsum(lengths), jnp.arange(rows * top), side="right").astype(jnp.int32)
    table = members.reshape(top, rows).T
    table = table[jax.random.permutation(jax.random.fold_in(own, 1), rows)]
    rotation = jax.random.randint(jax.random.fold_in(own, 2), (rows, 1), 0, top)
    return jnp.take_along_axis(table, (jnp.arange(top)[None, :] + rotation) % top, axis=1)


def portions_of(amount, total, most, slope, full):
    portions = [(1 << 20) // math.isqrt(rank ** slope) + 1 for rank in range(1, amount + 1)]
    largest = most if full else min(most, max(-(-total // amount), total * portions[0] // sum(portions)))
    least = 1 if total - largest >= amount - 1 else 0
    counts, rest = [largest] + [least] * (amount - 1), total - largest - least * (amount - 1)
    while rest > 0:
        candidates = [i for i in range(1, amount) if counts[i] < largest] or [i for i in range(1, amount) if counts[i] < most]
        pool, left = sum([portions[i] for i in candidates]), rest
        for i in candidates:
            extra = min(most - counts[i], max(1, left * portions[i] // pool), rest)
            counts[i] = counts[i] + extra
            rest = rest - extra
    return np.array(counts)


def bell_draw(own_key, shape, scale, most, split=(), kind=jnp.bfloat16):
    array = jax.random.normal(own_key, shape, jnp.float32) * scale
    if len(split) > 0:
        array = block_scale(own_key, shape, split, -0.22, 0.18) * array
    return jnp.clip(array, min=-most, max=most).astype(kind)


def heavy_noise(own_key, shape, scale, reach, shards, heavy, kind=jnp.bfloat16):
    array = scale * jax.random.normal(own_key, shape, jnp.float32)
    if shards:
        array = array * block_scale(own_key, shape, shards, -0.22, 0.18)
    return jnp.clip(spiked(array, jax.random.fold_in(own_key, 3), *heavy), -reach, reach).astype(kind)


def setup_inputs(seed: int = 0) -> dict:
    splits = jax.random.split(jax.random.key(seed), 10)
    hidden = heavy_noise(splits[0], (SECTIONS, TOKENS, D), 1.0, 6.0, ((0, 8), (1, 32)), (1, 2, 32, 2.75))
    expert_ids_keys = jax.random.split(jax.random.fold_in(splits[1], 1), SECTIONS * TOKENS // TOK_DEV)
    expert_ids_turns = jax.random.permutation(jax.random.fold_in(splits[1], 3), SECTIONS * TOKENS // TOK_DEV)
    expert_ids = jax.vmap(lambda own, number: deal_out(jax.random.fold_in(splits[1], 2), own, number, TOK_DEV, EXPERTS, 2, CAP, 2))(expert_ids_keys, expert_ids_turns).reshape((SECTIONS, TOKENS, 2))
    cotangent = bell_draw(splits[2], (SECTIONS, TOKENS, D), 1.0, 6.0, ((0, 8), (1, 32)))
    skip_weight = bell_draw(splits[3], (SECTIONS, 2 * D, D), (2 * D) ** -0.5, 0.125, ((0, 8),))
    norm_gain = jnp.clip(1.0 + 0.15 * jax.random.normal(splits[4], (SECTIONS, D), jnp.float32), 0.25, 1.75)
    router_weight = bell_draw(splits[5], (SECTIONS, D, EXPERTS), D ** -0.5, 0.1875, ((0, 8),))
    gate_weight = bell_draw(splits[6], (SECTIONS, EXPERTS, D, FF), D ** -0.5, 0.1875, ((0, 8), (1, 8)))
    up_weight = bell_draw(splits[7], (SECTIONS, EXPERTS, D, FF), D ** -0.5, 0.1875, ((0, 8), (1, 8)))
    down_weight = bell_draw(splits[8], (SECTIONS, EXPERTS, FF, D), FF ** -0.5, 0.1875, ((0, 8), (1, 8)))
    return {"hidden": hidden, "expert_ids": expert_ids, "cotangent": cotangent, "skip_weight": skip_weight, "norm_gain": norm_gain, "router_weight": router_weight, "gate_weight": gate_weight, "up_weight": up_weight, "down_weight": down_weight}


norm_eps = 1e-06

def matmul(left, right):
    return jnp.dot(left, right, preferred_element_type=jnp.float32)

def matmul_right_t(left, right):
    return lax.dot_general(left, right, (((1,), (1,)), ((), ())), preferred_element_type=jnp.float32)

def inner_rows(left, right):
    return lax.dot_general(left, right, (((0,), (0,)), ((), ())), preferred_element_type=jnp.float32)

def dispatch_index(expert_ids, experts, capacity):
    flat_ids = expert_ids.reshape(-1)
    expert_names = jnp.arange(experts, dtype=jnp.int32)
    onehot = (flat_ids[:, None] == expert_names[None, :]).astype(jnp.int32)
    before = jnp.cumsum(onehot, axis=0) - onehot
    return (flat_ids * capacity + lax.optimization_barrier(jnp.sum(before * onehot, axis=1))).astype(jnp.int32)

def place_rows(row_block, target, slot_total):
    width = row_block.shape[-1]
    return jnp.zeros((slot_total, width), row_block.dtype).at[target].set(row_block)

def section_front(own_rows, partner, expert_ids, skip_weight, norm_gain, router_weight, capacity):
    experts = router_weight.shape[1]
    joined = jnp.concatenate([own_rows, partner], axis=1)
    wide_rows = matmul(joined, skip_weight).astype(jnp.bfloat16).astype(jnp.float32)
    inv_rms = lax.rsqrt(lax.optimization_barrier(jnp.mean(wide_rows * wide_rows, axis=1, keepdims=True)) + norm_eps)
    normed = (wide_rows * inv_rms * norm_gain[None, :]).astype(jnp.bfloat16)
    logits = matmul(normed, router_weight)
    expert_names = jnp.arange(experts, dtype=jnp.int32)
    chosen = (expert_ids[:, :, None] == expert_names[None, None, :]).astype(jnp.float32)
    picked = lax.optimization_barrier(jnp.sum(chosen * logits[:, None, :], axis=2))
    scores = jax.nn.sigmoid(picked)
    weights = scores / lax.optimization_barrier(jnp.sum(scores, axis=1, keepdims=True))
    target = dispatch_index(expert_ids, experts, capacity)
    return (joined, wide_rows, inv_rms, normed, chosen, scores, weights, target)

def expert_forward(row_block, w_gate, w_up, w_down):
    gate_pre = matmul(row_block, w_gate)
    up_pre = matmul(row_block, w_up)
    act = (jax.nn.silu(gate_pre) * up_pre).astype(jnp.bfloat16)
    return (matmul(act, w_down).astype(jnp.bfloat16), gate_pre, up_pre)

def expert_backward(grad_rows, gate_pre, up_pre, w_gate, w_up, w_down):
    grad_act = matmul_right_t(grad_rows, w_down)
    sigmoid_gate = jax.nn.sigmoid(gate_pre)
    grad_gate = (grad_act * up_pre * sigmoid_gate * (1.0 + gate_pre * (1.0 - sigmoid_gate))).astype(jnp.bfloat16)
    grad_up = (grad_act * gate_pre * sigmoid_gate).astype(jnp.bfloat16)
    return (matmul_right_t(grad_gate, w_gate) + matmul_right_t(grad_up, w_up)).astype(jnp.bfloat16)

def section_back(grad_out, picked_out, weights, scores, chosen, grad_picked, normed, wide_rows, inv_rms, norm_gain, router_weight, skip_weight):
    picked_wide = picked_out.astype(jnp.float32)
    grad_weight = lax.optimization_barrier(jnp.sum(grad_out[:, None, :] * picked_wide, axis=2))
    weighted_sum = lax.optimization_barrier(jnp.sum(weights * grad_weight, axis=1, keepdims=True))
    grad_score = (grad_weight - weighted_sum) / lax.optimization_barrier(jnp.sum(scores, axis=1, keepdims=True))
    grad_picked_logit = grad_score * scores * (1.0 - scores)
    grad_logits = lax.optimization_barrier(jnp.sum(chosen * grad_picked_logit[:, :, None], axis=1)).astype(jnp.bfloat16)
    router_term = inner_rows(normed, grad_logits)
    grad_normed = lax.optimization_barrier(jnp.sum(grad_picked.astype(jnp.float32), axis=1)) + matmul_right_t(grad_logits, router_weight)
    unit_rows = wide_rows * inv_rms
    gain_term = lax.optimization_barrier(jnp.sum(grad_normed * unit_rows, axis=0))
    grad_unit = grad_normed * norm_gain[None, :]
    grad_mixed = (grad_out + inv_rms * (grad_unit - unit_rows * lax.optimization_barrier(jnp.mean(grad_unit * unit_rows, axis=1, keepdims=True)))).astype(jnp.bfloat16)
    grad_joined = matmul_right_t(grad_mixed, skip_weight).astype(jnp.bfloat16)
    return (grad_mixed, router_term, gain_term, grad_joined)

def reference(hidden, expert_ids, cotangent, skip_weight, norm_gain, router_weight, gate_weight, up_weight, down_weight):
    blocks = N_EXPERT * N_DP
    slot_total = EXPERTS * CAP
    half = SECTIONS // 2
    outs_list, own_list, mirror_list, skip_list, router_list, gain_list = ([], [], [], [], [], [])

    def run_forward(pack):
        return expert_forward(pack[0], pack[1], pack[2], pack[3])

    def run_backward(pack):
        return expert_backward(pack[0], pack[1], pack[2], pack[3], pack[4], pack[5])

    def to_experts(buffer):
        return buffer.reshape(blocks, EXPERTS, CAP, D).transpose(1, 0, 2, 3).reshape(EXPERTS, blocks * CAP, D)

    def to_blocks(buffer):
        return buffer.reshape(EXPERTS, blocks, CAP, D).transpose(1, 0, 2, 3).reshape(blocks, slot_total, D)
    for section in range(SECTIONS):
        own_rows = hidden[section].reshape(blocks, TOK_DEV, D)
        if section >= half:
            partner = hidden[SECTIONS - 1 - section].reshape(blocks, TOK_DEV, D)
        else:
            partner = jnp.zeros_like(own_rows)
        route_block = expert_ids[section].reshape(blocks, TOK_DEV, 2)
        front = jax.vmap(section_front, in_axes=(0, 0, 0, None, None, None, None))
        joined, wide_rows, inv_rms, normed, chosen, scores, weights, target = front(own_rows, partner, route_block, skip_weight[section], norm_gain[section], router_weight[section], CAP)
        placer = jax.vmap(place_rows, in_axes=(0, 0, None))
        send = placer(jnp.repeat(normed, 2, axis=1), target, slot_total)
        outputs, gate_pre, up_pre = lax.map(run_forward, (to_experts(send), gate_weight[section], up_weight[section], down_weight[section]))
        returned = to_blocks(outputs)
        picked_out = jnp.take_along_axis(returned, target[:, :, None], axis=1).reshape(blocks, TOK_DEV, 2, D)
        result = (wide_rows + lax.optimization_barrier(jnp.sum(weights[:, :, :, None] * picked_out.astype(jnp.float32), axis=2))).astype(jnp.bfloat16)
        grad_out = cotangent[section].reshape(blocks, TOK_DEV, D).astype(jnp.float32)
        grad_sent = (weights[:, :, :, None] * grad_out[:, :, None, :]).astype(jnp.bfloat16).reshape(blocks, 2 * TOK_DEV, D)
        grad_buffer = placer(grad_sent, target, slot_total)
        grad_inputs = lax.map(run_backward, (to_experts(grad_buffer), gate_pre, up_pre, gate_weight[section], up_weight[section], down_weight[section]))
        grad_back = to_blocks(grad_inputs)
        grad_picked = jnp.take_along_axis(grad_back, target[:, :, None], axis=1).reshape(blocks, TOK_DEV, 2, D)
        backer = jax.vmap(section_back, in_axes=(0, 0, 0, 0, 0, 0, 0, 0, 0, None, None, None))
        grad_mixed, router_term, gain_term, grad_joined = backer(grad_out, picked_out, weights, scores, chosen, grad_picked, normed, wide_rows, inv_rms, norm_gain[section], router_weight[section], skip_weight[section])
        skip_list.append(inner_rows(joined.reshape(TOKENS, 2 * D), grad_mixed.reshape(TOKENS, D)))
        router_list.append(lax.optimization_barrier(jnp.sum(router_term, axis=0)))
        gain_list.append(lax.optimization_barrier(jnp.sum(gain_term, axis=0)))
        outs_list.append(result.reshape(TOKENS, D))
        grad_joined = grad_joined.reshape(TOKENS, 2 * D)
        own_list.append(grad_joined[:, :D])
        mirror_list.append(grad_joined[:, D:])
    grads = []
    for section in range(SECTIONS):
        total = own_list[section].astype(jnp.float32)
        if section < half:
            total = total + mirror_list[SECTIONS - 1 - section].astype(jnp.float32)
        grads.append(total.astype(jnp.bfloat16))
    return (jnp.stack(outs_list), jnp.stack(grads), jnp.stack(skip_list), jnp.stack(router_list), jnp.stack(gain_list))
```

```python
import functools

import jax
import jax.numpy as jnp
from jax import lax
from jax.experimental import pallas as pl
from jax.experimental.pallas import tpu as pltpu
from jax.sharding import PartitionSpec as P

norm_eps = 1e-06
MESH = pl.DeviceIdType.MESH
BF = jnp.bfloat16
F32 = jnp.float32


def dot(left, right):
    return jnp.dot(left, right, preferred_element_type=F32)


def dot_rt(left, right):
    return lax.dot_general(left, right, (((1,), (1,)), ((), ())), preferred_element_type=F32)


def dot_lt(left, right):
    return lax.dot_general(left, right, (((0,), (0,)), ((), ())), preferred_element_type=F32)


def loop(count, body):
    for i in range(count):
        body(i)


class Copies:
    def __init__(self, send_sems, recv_sems):
        self.send_sems, self.recv_sems, self.used = send_sems, recv_sems, 0

    def make(self, src, dst, device):
        k = self.used
        self.used += 1
        return pltpu.make_async_remote_copy(
            src_ref=src,
            dst_ref=dst,
            send_sem=self.send_sems.at[k],
            recv_sem=self.recv_sems.at[k],
            device_id=device,
            device_id_type=MESH,
        )


N_SEM = 80


def kernel(
    hid, ids, cot, gain, rw, skip_h, gate_h, up_h, down_h,
    out_o, hg_o, sg_o, rg_o, gg_o,
    skip_v, gate_v, up_v, down_v,
    mir, hid_x, mir_x, jt,
    a0, a1, sl,
    gsend, grecv, nsend, nrecv, osend, orecv, bsend, brecv,
    ga, act, gg, gu,
    acc, normed, gn,
    rgs, rgx, rgr, rgy, rgf, rgo,
    gmh, gmx, gm2,
    mgs, mgr, own_g,
    pa, ra, pa2, ra2, pb, rb, pb2, rb2, fin, fin_x,
    local_sems, send_sems, recv_sems,
):
    T, D = hid.shape
    FF = gate_v.shape[1]
    E = 8
    CAP = nsend.shape[1]
    HALF = E // 2 * CAP
    W = D // 4
    H = D // 2
    n_sec = lax.axis_size("section")
    s = lax.axis_index("section")
    e = lax.axis_index("expert")
    d = lax.axis_index("dp")
    x, yh = e // 2, e % 2
    yl, c = d // 2, d % 2
    y = yh * 2 + yl
    upper = s >= n_sec // 2
    lower = s < n_sec // 2

    mirror_dev = (n_sec - 1 - s, e, d)
    core_dev = (s, e, d + 1 - 2 * c)

    def peer(dx, f):
        return (s, ((x + dx) % 4) * 2 + (yh + f) % 2, (d + 2 * f) % 4)

    def peer_y(dy):
        yy = (y + dy) % 4
        return (s, x * 2 + yy // 2, (yy % 2) * 2 + c)

    cp = Copies(send_sems, recv_sems)
    started = []

    def go(copy):
        copy.start()
        started.append(copy)

    loads = [
        pltpu.make_async_copy(src, dst, local_sems.at[i])
        for i, (src, dst) in enumerate(
            [(skip_h, skip_v), (down_h, down_v), (gate_h, gate_v), (up_h, up_v)]
        )
    ]
    for load in loads:
        load.start()

    barrier = pltpu.get_barrier_semaphore()
    greeted = [mirror_dev, core_dev]
    greeted += [peer(dx, f) for f in range(2) for dx in range(4) if (dx, f) != (0, 0)]
    greeted += [(s, e, (d + 2) % 4), (s, x * 2 + (yh + 1) % 2, d)]
    for device in greeted:
        pl.semaphore_signal(barrier, inc=1, device_id=device, device_id_type=MESH)
    pl.semaphore_wait(barrier, len(greeted))

    mirror_in = [cp.make(hid.at[:, pl.ds(j * W, W)], mir.at[j], mirror_dev) for j in range(4)]

    @pl.when(lower)
    def _():
        for copy in mirror_in:
            copy.start()

    hid_cp = cp.make(hid, hid_x, core_dev)
    go(hid_cp)

    def relative(names):
        dx = ((names >> 1) - x + 4) & 3
        f = ((names & 1) - yh + 2) & 1
        return f * 4 + dx

    id0, id1 = ids[:, 0:1], ids[:, 1:2]
    rel0, rel1 = relative(id0), relative(id1)
    lane = lax.broadcasted_iota(jnp.int32, (T, 128), 1)
    row = lax.broadcasted_iota(jnp.int32, (T, 128), 0)
    c0, c1 = rel0 == lane, rel1 == lane
    counts = jnp.where(c0, 1.0, 0.0) + jnp.where(c1, 1.0, 0.0)
    earlier = jnp.where(lane < row, 1.0, 0.0).astype(BF)
    before = dot(earlier, counts.astype(BF))
    rank0 = jnp.sum(jnp.where(c0, before, 0.0), axis=1, keepdims=True)
    rank1 = jnp.sum(jnp.where(c1, before, 0.0), axis=1, keepdims=True)
    slots = lax.broadcasted_iota(jnp.int32, (T, E * CAP), 1).astype(F32)
    at0 = jnp.where(rel0.astype(F32) * CAP + rank0 == slots, 1.0, 0.0)
    at1 = jnp.where(rel1.astype(F32) * CAP + rank1 == slots, 1.0, 0.0)
    a0[...] = at0.astype(BF)
    a1[...] = at1.astype(BF)
    eye = jnp.where(lane == row, 1.0, 0.0).astype(BF)
    sl[...] = dot_lt((at0 + at1).astype(BF), eye).astype(BF)

    order = [(2, 1), (2, 0), (1, 1), (3, 1), (1, 0), (3, 0), (0, 1)]

    def label(dx, f):
        return f * 4 + dx

    def place(rows, send, recv):
        def tile(i):
            cols = pl.ds(i * W, W)
            placed = dot(sl[...], rows[:, cols]).astype(BF)
            for o in range(E):
                block = placed[o * CAP : (o + 1) * CAP, :]
                if o == 0:
                    recv[0, :, cols] = block
                else:
                    send[o, :, cols] = block

        loop(D // W, tile)

    def dispatch(send, recv):
        copies = {}
        for dx, f in order:
            o = label(dx, f)
            copies[o] = cp.make(send.at[o], recv.at[o], peer(dx, f))
            go(copies[o])
        return copies

    def give_back(send, recv, copies, f):
        for dx, ff in order:
            if ff == f:
                o = label(dx, ff)
                copies[o] = cp.make(send.at[o], recv.at[o], peer((4 - dx) % 4, f))
                go(copies[o])

    place(cot, gsend, grecv)
    g_cp = dispatch(gsend, grecv)

    loads[0].wait()

    def own_mix(i):
        cols = pl.ds(i * W, W)
        acc[:, cols] = dot(hid[...], skip_v[0:D, cols])

    loop(D // W, own_mix)

    def turn(rows, at, col0):
        jt[pl.ds(at, rows.shape[1]), pl.ds(col0, T)] = rows.T

    loop(4, lambda j: turn(hid[:, j * W : (j + 1) * W], j * W, 0))
    hid_cp.wait_recv()
    loop(4, lambda j: turn(hid_x[:, j * W : (j + 1) * W], j * W, T))

    loads[1].wait()
    for o in g_cp:
        g_cp[o].wait_recv()

    def grad_act(i):
        cols = pl.ds(i * W, W)
        rows = grecv[...].reshape(E * CAP, D)
        ga[:, cols] = dot_rt(rows, down_v[cols, :])

    loop(FF // W, grad_act)

    mir_cp = cp.make(mir, mir_x, core_dev)

    @pl.when(upper)
    def _():
        for j in range(4):
            mirror_in[j].wait_recv()

            def add_mix(i, j=j):
                cols = pl.ds(i * W, W)
                acc[:, cols] += dot(mir[j], skip_v[D + j * W : D + (j + 1) * W, cols])

            loop(D // W, add_mix)
        mir_cp.start()

    wide = acc[...].astype(BF).astype(F32)
    acc[...] = wide
    inv_rms = lax.rsqrt(jnp.mean(wide * wide, axis=1, keepdims=True) + norm_eps)
    normed[...] = (wide * inv_rms * gain[...]).astype(BF)

    place(normed, nsend, nrecv)
    n_cp = dispatch(nsend, nrecv)

    lane8 = lax.broadcasted_iota(jnp.int32, (T, 8), 1)
    k0, k1 = id0 == lane8, id1 == lane8
    logits = dot(normed[...], rw[...])
    s0 = jax.nn.sigmoid(jnp.sum(jnp.where(k0, logits, 0.0), axis=1, keepdims=True))
    s1 = jax.nn.sigmoid(jnp.sum(jnp.where(k1, logits, 0.0), axis=1, keepdims=True))
    total = s0 + s1
    w0, w1 = s0 / total, s1 / total

    @pl.when(upper)
    def _():
        loop(4, lambda j: turn(mir[j], D + j * W, 0))

    @pl.when(lower)
    def _():
        jt[D : 2 * D, :] = jnp.zeros((D, 2 * T), BF)

    loads[2].wait()
    loads[3].wait()

    o_cp, b_cp = {}, {}
    for f in range(2):
        blocks = slice(f * 4, f * 4 + 4)
        rows = slice(f * HALF, (f + 1) * HALF)
        for o in range(f * 4, f * 4 + 4):
            if o != 0:
                n_cp[o].wait_recv()

        def hidden_units(i):
            cols = pl.ds(i * W, W)
            frames = nrecv[blocks].reshape(HALF, D)
            pre_gate = dot(frames, gate_v[:, cols])
            pre_up = dot(frames, up_v[:, cols])
            grad = ga[rows, cols]
            sig = jax.nn.sigmoid(pre_gate)
            silu = pre_gate * sig
            act[rows, cols] = (silu * pre_up).astype(BF)
            gg[rows, cols] = (grad * pre_up * sig * (1.0 + pre_gate * (1.0 - sig))).astype(BF)
            gu[rows, cols] = (grad * silu).astype(BF)

        loop(FF // W, hidden_units)

        def split(values, send, recv, cols):
            for k in range(4):
                block = values[k * CAP : (k + 1) * CAP, :]
                if f == 0 and k == 0:
                    recv[0, :, cols] = block
                else:
                    send[f * 4 + k, :, cols] = block

        def outputs(i):
            cols = pl.ds(i * W, W)
            split(dot(act[rows, :], down_v[:, cols]).astype(BF), osend, orecv, cols)

        loop(D // W, outputs)
        give_back(osend, orecv, o_cp, f)

        def inputs(i):
            cols = pl.ds(i * W, W)
            grads = dot_rt(gg[rows, :], gate_v[cols, :]) + dot_rt(gu[rows, :], up_v[cols, :])
            split(grads.astype(BF), bsend, brecv, cols)

        loop(D // W, inputs)
        give_back(bsend, brecv, b_cp, f)

    @pl.when(upper)
    def _():
        mir_cp.wait_recv()
        loop(4, lambda j: turn(mir_x[j], D + j * W, T))

    for o in o_cp:
        o_cp[o].wait_recv()
    grad_w0, grad_w1 = 0.0, 0.0
    for i in range(D // W):
        cols = slice(i * W, (i + 1) * W)
        rows_o = orecv[:, :, cols].reshape(E * CAP, W)
        p0, p1 = dot(a0[...], rows_o), dot(a1[...], rows_o)
        out_o[:, cols] = (acc[:, cols] + w0 * p0 + w1 * p1).astype(BF)
        grad_out = cot[:, cols].astype(F32)
        grad_w0 += jnp.sum(grad_out * p0, axis=1, keepdims=True)
        grad_w1 += jnp.sum(grad_out * p1, axis=1, keepdims=True)
    weighted = w0 * grad_w0 + w1 * grad_w1
    gl0 = (grad_w0 - weighted) / total * s0 * (1.0 - s0)
    gl1 = (grad_w1 - weighted) / total * s1 * (1.0 - s1)
    grad_logits = (jnp.where(k0, gl0, 0.0) + jnp.where(k1, gl1, 0.0)).astype(BF)

    for o in b_cp:
        b_cp[o].wait_recv()
    mean_term = 0.0
    for i in range(D // W):
        cols = slice(i * W, (i + 1) * W)
        rows_b = brecv[:, :, cols].reshape(E * CAP, W)
        grad_normed = w0 * dot(a0[...], rows_b) + w1 * dot(a1[...], rows_b)
        grad_normed += dot_rt(grad_logits, rw[cols, :])
        unit = acc[:, cols] * inv_rms
        gain_term = jnp.sum(grad_normed * unit, axis=0, keepdims=True)
        router_term = dot_lt(grad_logits, normed[:, cols])
        both = jnp.concatenate([router_term, jnp.broadcast_to(gain_term, (8, W))], axis=0)
        rgs[i // 2, :, (i % 2) * W : (i % 2 + 1) * W] = both.astype(BF)
        grad_unit = grad_normed * gain[:, cols]
        gn[:, cols] = grad_unit
        mean_term += jnp.sum(grad_unit * unit, axis=1, keepdims=True)
    mean_term = mean_term / D
    rg_core = cp.make(rgs.at[1 - c], rgx, core_dev)
    go(rg_core)
    for i in range(D // W):
        cols = slice(i * W, (i + 1) * W)
        unit = acc[:, cols] * inv_rms
        grad_mixed = cot[:, cols].astype(F32) + inv_rms * (gn[:, cols] - unit * mean_term)
        gmh[i // 2, :, (i % 2) * W : (i % 2 + 1) * W] = grad_mixed.astype(BF)
    gm_core = cp.make(gmh.at[1 - c], gmx, core_dev)
    go(gm_core)

    grad_mixed = jnp.concatenate([gmh[0], gmh[1]], axis=1)

    mirror_out = [cp.make(mgs.at[j], mgr.at[j], mirror_dev) for j in range(4)]

    @pl.when(upper)
    def _():
        for j in range(4):
            mgs[j] = dot_rt(grad_mixed, skip_v[D + j * W : D + (j + 1) * W, :]).astype(BF)
            mirror_out[j].start()

    rg_core.wait_recv()
    rgr[x] = (rgs[c].astype(F32) + rgx[...].astype(F32)).astype(BF)
    rg_x = [cp.make(rgr.at[x], rgr.at[x], peer(dx, 0)) for dx in (2, 1, 3)]
    for copy in rg_x:
        go(copy)

    gm_core.wait_recv()
    gm2[0:T, :] = gmh[c]
    gm2[T : 2 * T, :] = gmx[...]
    a1_cp, b1_cp = {}, {}
    for dx in (2, 1, 3, 0):
        xx = (x + dx) % 4
        part = dot(jt[pl.ds(pl.multiple_of(xx * 4 * T, 4 * T), 4 * T), :], gm2[...])
        pa[dx] = part[:, :W].astype(BF)
        for yy in range(4):
            pb[yy, dx] = part[yy * T : (yy + 1) * T, W:].astype(BF)
        if dx != 0:
            a1_cp[dx] = cp.make(pa.at[dx], ra.at[dx], peer(dx, 0))
            go(a1_cp[dx])
    for dy in (2, 1, 3):
        b1_cp[dy] = cp.make(pb.at[(y + dy) % 4], rb.at[dy], peer_y(dy))
        go(b1_cp[dy])

    def own_grad(j):
        cols = pl.ds(j * W, W)
        own_g[:, cols] = dot_rt(grad_mixed, skip_v[cols, :]).astype(BF)

    loop(4, own_grad)

    for copy in rg_x:
        copy.wait_recv()
    sum_x = rgr[0].astype(F32) + rgr[1].astype(F32) + rgr[2].astype(F32) + rgr[3].astype(F32)
    rgy[y] = sum_x.astype(BF)
    rg_y = [cp.make(rgy.at[y], rgy.at[y], peer_y(dy)) for dy in (2, 1, 3)]
    for copy in rg_y:
        go(copy)

    for dx in (1, 3, 2):
        a1_cp[dx].wait_recv()
    sum_a = pa[0].astype(F32) + ra[1].astype(F32) + ra[2].astype(F32) + ra[3].astype(F32)
    for yy in range(4):
        pa2[yy] = sum_a[yy * T : (yy + 1) * T, :].astype(BF)
    a2_cp = {}
    for dy in (2, 1, 3):
        a2_cp[dy] = cp.make(pa2.at[(y + dy) % 4], ra2.at[dy], peer_y(dy))
        go(a2_cp[dy])
    for dy in (1, 3, 2):
        b1_cp[dy].wait_recv()
    b2_cp = {}
    for dx in (2, 1, 3, 0):
        sum_b = pb[y, dx].astype(F32)
        for dy in (1, 2, 3):
            sum_b += rb[dy, dx].astype(F32)
        pb2[dx] = sum_b.astype(BF)
        if dx != 0:
            b2_cp[dx] = cp.make(pb2.at[dx], rb2.at[dx], peer(dx, 0))
            go(b2_cp[dx])

    for copy in rg_y:
        copy.wait_recv()
    rgf[...] = rgy[0].astype(F32) + rgy[1].astype(F32) + rgy[2].astype(F32) + rgy[3].astype(F32)
    rg_out = cp.make(rgf, rgo, core_dev)
    go(rg_out)

    for dy in (1, 3, 2):
        a2_cp[dy].wait_recv()
    res_a = pa2[y].astype(F32)
    for dy in (1, 2, 3):
        res_a += ra2[dy].astype(F32)
    for dx in (1, 3, 2):
        b2_cp[dx].wait_recv()
    res_b = pb2[0].astype(F32)
    for dx in (1, 2, 3):
        res_b += rb2[dx].astype(F32)
    for h in range(2):
        fin[h, :, 0:W] = res_a[h * (T // 2) : (h + 1) * (T // 2), :]
        fin[h, :, W:H] = res_b[h * (T // 2) : (h + 1) * (T // 2), :]
    fin_cp = cp.make(fin.at[1 - c], fin_x, core_dev)
    go(fin_cp)

    @pl.when(upper)
    def _():
        hg_o[...] = own_g[...]

    @pl.when(lower)
    def _():
        for j in range(4):
            mirror_out[j].wait_recv()
            cols = slice(j * W, (j + 1) * W)
            hg_o[:, cols] = (own_g[:, cols].astype(F32) + mgr[j].astype(F32)).astype(BF)

    here = pl.ds(pl.multiple_of(c * H, H), H)
    there = pl.ds(pl.multiple_of((1 - c) * H, H), H)
    rg_out.wait_recv()
    rg_o[:, here] = rgf[0:8, :]
    rg_o[:, there] = rgo[0:8, :]
    gg_o[:, here] = rgf[8:9, :]
    gg_o[:, there] = rgo[8:9, :]
    fin_cp.wait_recv()
    sg_o[:, here] = fin[c]
    sg_o[:, there] = fin_x[...]

    for copy in started:
        copy.wait_send()

    @pl.when(lower)
    def _():
        for copy in mirror_in:
            copy.wait_send()

    @pl.when(upper)
    def _():
        mir_cp.wait_send()
        for copy in mirror_out:
            copy.wait_send()


def per_device(
    hidden, expert_ids, cotangent, skip_weight, norm_gain, router_weight,
    gate_weight, up_weight, down_weight,
):
    T, D = hidden.shape[1:]
    FF = gate_weight.shape[-1]
    E = lax.axis_size("expert")
    CAP = min(T, 3 * T // E)
    W, H = D // 4, D // 2
    slots = E * CAP
    vmem = pl.BlockSpec(memory_space=pltpu.VMEM)
    anywhere = pl.BlockSpec(memory_space=pl.ANY)
    a2a = pltpu.VMEM((E, CAP, D), BF)
    scratch = [
        pltpu.VMEM((2 * D, D), BF), pltpu.VMEM((D, FF), BF), pltpu.VMEM((D, FF), BF), pltpu.VMEM((FF, D), BF),
        pltpu.VMEM((4, T, W), BF), pltpu.VMEM((T, D), BF), pltpu.VMEM((4, T, W), BF), pltpu.VMEM((2 * D, 2 * T), BF),
        pltpu.VMEM((T, slots), BF), pltpu.VMEM((T, slots), BF), pltpu.VMEM((slots, T), BF),
        a2a, a2a, a2a, a2a, a2a, a2a, a2a, a2a,
        pltpu.VMEM((slots, FF), F32), pltpu.VMEM((slots, FF), BF), pltpu.VMEM((slots, FF), BF), pltpu.VMEM((slots, FF), BF),
        pltpu.VMEM((T, D), F32), pltpu.VMEM((T, D), BF), pltpu.VMEM((T, D), F32),
        pltpu.VMEM((2, 16, H), BF), pltpu.VMEM((16, H), BF), pltpu.VMEM((4, 16, H), BF), pltpu.VMEM((4, 16, H), BF),
        pltpu.VMEM((16, H), F32), pltpu.VMEM((16, H), F32),
        pltpu.VMEM((2, T, H), BF), pltpu.VMEM((T, H), BF), pltpu.VMEM((2 * T, H), BF),
        pltpu.VMEM((4, T, W), BF), pltpu.VMEM((4, T, W), BF), pltpu.VMEM((T, D), BF),
        pltpu.VMEM((4, 4 * T, W), BF), pltpu.VMEM((4, 4 * T, W), BF), pltpu.VMEM((4, T, W), BF), pltpu.VMEM((4, T, W), BF),
        pltpu.VMEM((4, 4, T, W), BF), pltpu.VMEM((4, 4, T, W), BF), pltpu.VMEM((4, T, W), BF), pltpu.VMEM((4, T, W), BF),
        pltpu.VMEM((2, T // 2, H), F32), pltpu.VMEM((T // 2, H), F32),
        pltpu.SemaphoreType.DMA((4,)), pltpu.SemaphoreType.DMA((N_SEM,)), pltpu.SemaphoreType.DMA((N_SEM,)),
    ]
    out, hidden_grad, skip_grad, router, gain = pl.pallas_call(
        kernel,
        out_shape=(
            jax.ShapeDtypeStruct((T, D), BF),
            jax.ShapeDtypeStruct((T, D), BF),
            jax.ShapeDtypeStruct((T // 2, D), F32),
            jax.ShapeDtypeStruct((8, D), F32),
            jax.ShapeDtypeStruct((1, D), F32),
        ),
        in_specs=[vmem] * 5 + [anywhere] * 4,
        out_specs=[vmem] * 5,
        scratch_shapes=scratch,
        compiler_params=pltpu.CompilerParams(
            collective_id=0, has_side_effects=True, vmem_limit_bytes=60 * 1024 * 1024
        ),
    )(
        hidden[0], expert_ids[0], cotangent[0], norm_gain, router_weight[0],
        skip_weight[0], gate_weight[0, 0], up_weight[0, 0], down_weight[0, 0],
    )
    return (out[None], hidden_grad[None], skip_grad[None], router.T[None], gain)


def solution(mesh):
    return jax.shard_map(
        per_device,
        mesh=mesh,
        in_specs=(
            P("section", ("expert", "dp"), None),
            P("section", ("expert", "dp"), None),
            P("section", ("expert", "dp"), None),
            P("section", None, None),
            P("section", None),
            P("section", None, None),
            P("section", "expert", None, None),
            P("section", "expert", None, None),
            P("section", "expert", None, None),
        ),
        out_specs=(
            P("section", ("expert", "dp"), None),
            P("section", ("expert", "dp"), None),
            P("section", ("expert", "dp"), None),
            P("section", None, None),
            P("section", None),
        ),
        check_vma=False,
    )
```

```python
import functools

import jax
import jax.numpy as jnp
from jax import lax
from jax.experimental import pallas as pl
from jax.experimental.pallas import tpu as pltpu
from jax.sharding import PartitionSpec as P

norm_eps = 1e-06
MESH = pl.DeviceIdType.MESH
BF = jnp.bfloat16
F32 = jnp.float32


def dot(left, right):
    return jnp.dot(left, right, preferred_element_type=F32)


def dot_rt(left, right):
    return lax.dot_general(left, right, (((1,), (1,)), ((), ())), preferred_element_type=F32)


def dot_lt(left, right):
    return lax.dot_general(left, right, (((0,), (0,)), ((), ())), preferred_element_type=F32)


def loop(count, body):
    for i in range(count):
        body(i)


class Copies:
    def __init__(self, send_sems, recv_sems):
        self.send_sems, self.recv_sems, self.used = send_sems, recv_sems, 0

    def make(self, src, dst, device):
        k = self.used
        self.used += 1
        return pltpu.make_async_remote_copy(
            src_ref=src,
            dst_ref=dst,
            send_sem=self.send_sems.at[k],
            recv_sem=self.recv_sems.at[k],
            device_id=device,
            device_id_type=MESH,
        )


N_SEM = 80


def kernel(
    hid, ids, cot, gain, rw, skip_h, gate_h, up_h, down_h,
    out_o, hg_o, sg_o, rg_o, gg_o,
    skip_v, gate_v, up_v, down_v,
    mir, hid_x, mir_x, jt,
    a0, a1, sl,
    gsend, grecv, nsend, nrecv, osend, orecv, bsend, brecv, wsend, wrecv,
    ga, act, gg, gu,
    acc, normed, gn,
    rgs, rgx, rgr, rgy, rgf, rgo,
    gmh, gmx, gm2,
    mgs, mgr, own_g,
    pa, ra, pa2, ra2, pb, rb, pb2, rb2, fin, fin_x,
    local_sems, send_sems, recv_sems,
):
    T, D = hid.shape
    FF = gate_v.shape[1]
    E = 8
    CAP = nsend.shape[1]
    HALF = E // 2 * CAP
    W = D // 4
    H = D // 2
    n_sec = lax.axis_size("section")
    s = lax.axis_index("section")
    e = lax.axis_index("expert")
    d = lax.axis_index("dp")
    x, yh = e // 2, e % 2
    yl, c = d // 2, d % 2
    y = yh * 2 + yl
    upper = s >= n_sec // 2
    lower = s < n_sec // 2

    mirror_dev = (n_sec - 1 - s, e, d)
    core_dev = (s, e, d + 1 - 2 * c)

    def peer(dx, f):
        return (s, ((x + dx) % 4) * 2 + (yh + f) % 2, (d + 2 * f) % 4)

    def peer_y(dy):
        yy = (y + dy) % 4
        return (s, x * 2 + yy // 2, (yy % 2) * 2 + c)

    cp = Copies(send_sems, recv_sems)
    started = []

    def go(copy):
        copy.start()
        started.append(copy)

    loads = [
        pltpu.make_async_copy(src, dst, local_sems.at[i])
        for i, (src, dst) in enumerate(
            [(skip_h, skip_v), (down_h, down_v), (gate_h, gate_v), (up_h, up_v)]
        )
    ]
    for load in loads:
        load.start()

    barrier = pltpu.get_barrier_semaphore()
    greeted = [mirror_dev, core_dev]
    greeted += [peer(dx, f) for f in range(2) for dx in range(4) if (dx, f) != (0, 0)]
    greeted += [(s, e, (d + 2) % 4), (s, x * 2 + (yh + 1) % 2, d)]
    for device in greeted:
        pl.semaphore_signal(barrier, inc=1, device_id=device, device_id_type=MESH)
    pl.semaphore_wait(barrier, len(greeted))

    mirror_in = [cp.make(hid.at[:, pl.ds(j * W, W)], mir.at[j], mirror_dev) for j in range(4)]

    @pl.when(lower)
    def _():
        for copy in mirror_in:
            copy.start()

    hid_cp = cp.make(hid, hid_x, core_dev)
    go(hid_cp)

    def relative(names):
        dx = ((names >> 1) - x + 4) & 3
        f = ((names & 1) - yh + 2) & 1
        return f * 4 + dx

    lane = lax.broadcasted_iota(jnp.int32, (T, 128), 1)
    row = lax.broadcasted_iota(jnp.int32, (T, 128), 0)
    eye = jnp.where(lane == row, 1.0, 0.0).astype(BF)
    names = dot_rt(eye, ids[...].astype(F32).astype(BF)).astype(jnp.int32)
    id0, id1 = names[:, 0:1], names[:, 1:2]
    rel0, rel1 = relative(id0), relative(id1)
    c0, c1 = rel0 == lane, rel1 == lane
    counts = jnp.where(c0, 1.0, 0.0) + jnp.where(c1, 1.0, 0.0)
    earlier = jnp.where(lane < row, 1.0, 0.0).astype(BF)
    before = dot(earlier, counts.astype(BF))
    rank0 = jnp.sum(jnp.where(c0, before, 0.0), axis=1, keepdims=True)
    rank1 = jnp.sum(jnp.where(c1, before, 0.0), axis=1, keepdims=True)
    slots = lax.broadcasted_iota(jnp.int32, (T, E * CAP), 1).astype(F32)
    at0 = jnp.where(rel0.astype(F32) * CAP + rank0 == slots, 1.0, 0.0)
    at1 = jnp.where(rel1.astype(F32) * CAP + rank1 == slots, 1.0, 0.0)
    a0[...] = at0.astype(BF)
    a1[...] = at1.astype(BF)
    sl[...] = dot_lt((at0 + at1).astype(BF), eye).astype(BF)

    order = [(2, 0), (1, 0), (3, 0), (2, 1), (1, 1), (3, 1), (0, 1)]

    def label(dx, f):
        return f * 4 + dx

    def place(rows, send, recv):
        def tile(i):
            cols = pl.ds(i * W, W)
            placed = dot(sl[...], rows[:, cols]).astype(BF)
            for o in range(E):
                block = placed[o * CAP : (o + 1) * CAP, :]
                if o == 0:
                    recv[0, :, cols] = block
                else:
                    send[o, :, cols] = block

        loop(D // W, tile)

    def dispatch(send, recv):
        copies = {}
        for dx, f in order:
            o = label(dx, f)
            copies[o] = cp.make(send.at[o], recv.at[o], peer(dx, f))
            go(copies[o])
        return copies

    def give_back(send, recv, copies, f):
        for dx, ff in order:
            if ff == f:
                o = label(dx, ff)
                copies[o] = cp.make(send.at[o], recv.at[o], peer((4 - dx) % 4, f))
                go(copies[o])

    place(cot, gsend, grecv)
    g_cp = dispatch(gsend, grecv)

    loads[0].wait()

    def own_mix(i):
        cols = pl.ds(i * W, W)
        acc[:, cols] = dot(hid[...], skip_v[0:D, cols])

    loop(D // W, own_mix)

    def turn(rows, at, col0):
        jt[pl.ds(at, rows.shape[1]), pl.ds(col0, T)] = rows.T

    loop(4, lambda j: turn(hid[:, j * W : (j + 1) * W], j * W, 0))
    hid_cp.wait_recv()
    loop(4, lambda j: turn(hid_x[:, j * W : (j + 1) * W], j * W, T))

    loads[1].wait()
    for o in g_cp:
        g_cp[o].wait_recv()

    def grad_act(i):
        cols = pl.ds(i * W, W)
        rows = grecv[...].reshape(E * CAP, D)
        ga[:, cols] = dot_rt(rows, down_v[cols, :])

    loop(FF // W, grad_act)

    mir_cp = cp.make(mir, mir_x, core_dev)

    @pl.when(upper)
    def _():
        for j in range(4):
            mirror_in[j].wait_recv()

            def add_mix(i, j=j):
                cols = pl.ds(i * W, W)
                acc[:, cols] += dot(mir[j], skip_v[D + j * W : D + (j + 1) * W, cols])

            loop(D // W, add_mix)
        mir_cp.start()

    wide = acc[...].astype(BF).astype(F32)
    acc[...] = wide
    inv_rms = lax.rsqrt(jnp.mean(wide * wide, axis=1, keepdims=True) + norm_eps)
    normed[...] = (wide * inv_rms * gain[...]).astype(BF)

    place(normed, nsend, nrecv)
    n_cp = dispatch(nsend, nrecv)

    lane8 = lax.broadcasted_iota(jnp.int32, (T, 8), 1)
    k0, k1 = id0 == lane8, id1 == lane8
    logits = dot_rt(normed[...], rw[...])
    s0 = jax.nn.sigmoid(jnp.sum(jnp.where(k0, logits, 0.0), axis=1, keepdims=True))
    s1 = jax.nn.sigmoid(jnp.sum(jnp.where(k1, logits, 0.0), axis=1, keepdims=True))
    total = s0 + s1
    w0, w1 = s0 / total, s1 / total

    @pl.when(upper)
    def _():
        loop(4, lambda j: turn(mir[j], D + j * W, 0))

    @pl.when(lower)
    def _():
        jt[D : 2 * D, :] = jnp.zeros((D, 2 * T), BF)

    loads[2].wait()
    loads[3].wait()

    def split(values, send, recv, cols, f):
        for k in range(4):
            block = values[k * CAP : (k + 1) * CAP, :]
            if f == 0 and k == 0:
                recv[0, :, cols] = block
            else:
                send[f * 4 + k, :, cols] = block

    o_cp, b_cp = {}, {}
    for f in range(2):
        blocks = slice(f * 4, f * 4 + 4)
        rows = slice(f * HALF, (f + 1) * HALF)
        for o in range(f * 4, f * 4 + 4):
            if o != 0:
                n_cp[o].wait_recv()

        def hidden_units(i):
            cols = pl.ds(i * W, W)
            frames = nrecv[blocks].reshape(HALF, D)
            pre_gate = dot(frames, gate_v[:, cols])
            pre_up = dot(frames, up_v[:, cols])
            grad = ga[rows, cols]
            sig = jax.nn.sigmoid(pre_gate)
            silu = pre_gate * sig
            act[rows, cols] = (silu * pre_up).astype(BF)
            gg[rows, cols] = (grad * pre_up * sig * (1.0 + pre_gate * (1.0 - sig))).astype(BF)
            gu[rows, cols] = (grad * silu).astype(BF)

        loop(FF // W, hidden_units)

        def inputs(i):
            cols = pl.ds(i * W, W)
            grads = dot_rt(gg[rows, :], gate_v[cols, :]) + dot_rt(gu[rows, :], up_v[cols, :])
            split(grads.astype(BF), bsend, brecv, cols, f)

        loop(D // W, inputs)
        give_back(bsend, brecv, b_cp, f)

    w_cp = {}
    for f in range(2):
        blocks = slice(f * 4, f * 4 + 4)
        rows = slice(f * HALF, (f + 1) * HALF)
        along = 0.0
        for i in range(D // W):
            cols = slice(i * W, (i + 1) * W)
            values = dot(act[rows, :], down_v[:, cols]).astype(BF)
            split(values, osend, orecv, cols, f)
            grads = grecv[blocks, :, cols].reshape(HALF, W).astype(F32)
            along += jnp.sum(values.astype(F32) * grads, axis=1, keepdims=True)
        high = along.astype(BF)
        low = (along - high.astype(F32)).astype(BF)
        half = lax.broadcasted_iota(jnp.int32, (HALF, 128), 1) < 64
        split(jnp.where(half, high, low), wsend, wrecv, slice(0, 128), f)
        give_back(wsend, wrecv, w_cp, f)
    for o in b_cp:
        b_cp[o].wait_send()
    for f in range(2):
        give_back(osend, orecv, o_cp, f)

    @pl.when(upper)
    def _():
        mir_cp.wait_recv()
        loop(4, lambda j: turn(mir_x[j], D + j * W, T))

    for o in w_cp:
        w_cp[o].wait_recv()
    rows_w = wrecv[...].reshape(E * CAP, 128)
    t0, t1 = dot(a0[...], rows_w), dot(a1[...], rows_w)
    grad_w0 = t0[:, 0:1] + t0[:, 64:65]
    grad_w1 = t1[:, 0:1] + t1[:, 64:65]
    weighted = w0 * grad_w0 + w1 * grad_w1
    gl0 = (grad_w0 - weighted) / total * s0 * (1.0 - s0)
    gl1 = (grad_w1 - weighted) / total * s1 * (1.0 - s1)
    grad_logits = (jnp.where(k0, gl0, 0.0) + jnp.where(k1, gl1, 0.0)).astype(BF)

    for o in b_cp:
        b_cp[o].wait_recv()
    mean_term = 0.0
    for i in range(D // W):
        cols = slice(i * W, (i + 1) * W)
        rows_b = brecv[:, :, cols].reshape(E * CAP, W)
        grad_normed = w0 * dot(a0[...], rows_b) + w1 * dot(a1[...], rows_b)
        grad_normed += dot(grad_logits, rw[:, cols])
        unit = acc[:, cols] * inv_rms
        gain_term = jnp.sum(grad_normed * unit, axis=0, keepdims=True)
        router_term = dot_lt(grad_logits, normed[:, cols])
        both = jnp.concatenate([router_term, jnp.broadcast_to(gain_term, (8, W))], axis=0)
        rgs[i // 2, :, (i % 2) * W : (i % 2 + 1) * W] = both.astype(BF)
        grad_unit = grad_normed * gain[:, cols]
        gn[:, cols] = grad_unit
        mean_term += jnp.sum(grad_unit * unit, axis=1, keepdims=True)
    mean_term = mean_term / D
    rg_core = cp.make(rgs.at[1 - c], rgx, core_dev)
    go(rg_core)
    for i in range(D // W):
        cols = slice(i * W, (i + 1) * W)
        unit = acc[:, cols] * inv_rms
        grad_mixed = cot[:, cols].astype(F32) + inv_rms * (gn[:, cols] - unit * mean_term)
        gmh[i // 2, :, (i % 2) * W : (i % 2 + 1) * W] = grad_mixed.astype(BF)
    gm_core = cp.make(gmh.at[1 - c], gmx, core_dev)
    go(gm_core)

    grad_mixed = jnp.concatenate([gmh[0], gmh[1]], axis=1)

    mirror_out = [cp.make(mgs.at[j], mgr.at[j], mirror_dev) for j in range(4)]

    @pl.when(upper)
    def _():
        for j in range(4):
            mgs[j] = dot_rt(grad_mixed, skip_v[D + j * W : D + (j + 1) * W, :]).astype(BF)
            mirror_out[j].start()

    rg_core.wait_recv()
    rgr[x] = (rgs[c].astype(F32) + rgx[...].astype(F32)).astype(BF)
    rg_x = [cp.make(rgr.at[x], rgr.at[x], peer(dx, 0)) for dx in (2, 1, 3)]
    for copy in rg_x:
        go(copy)

    gm_core.wait_recv()
    gm2[0:T, :] = gmh[c]
    gm2[T : 2 * T, :] = gmx[...]
    a1_cp, b1_cp = {}, {}
    for dx in (2, 1, 3, 0):
        xx = (x + dx) % 4
        part = dot(jt[pl.ds(pl.multiple_of(xx * 4 * T, 4 * T), 4 * T), :], gm2[...])
        pa[dx] = part[:, :W].astype(BF)
        for yy in range(4):
            pb[yy, dx] = part[yy * T : (yy + 1) * T, W:].astype(BF)
        if dx != 0:
            a1_cp[dx] = cp.make(pa.at[dx], ra.at[dx], peer(dx, 0))
            go(a1_cp[dx])
    for dy in (2, 1, 3):
        b1_cp[dy] = cp.make(pb.at[(y + dy) % 4], rb.at[dy], peer_y(dy))
        go(b1_cp[dy])

    def own_grad(j):
        cols = pl.ds(j * W, W)
        own_g[:, cols] = dot_rt(grad_mixed, skip_v[cols, :]).astype(BF)

    loop(4, own_grad)

    for o in o_cp:
        o_cp[o].wait_recv()
    for i in range(D // W):
        cols = slice(i * W, (i + 1) * W)
        rows_o = orecv[:, :, cols].reshape(E * CAP, W)
        p0, p1 = dot(a0[...], rows_o), dot(a1[...], rows_o)
        out_o[:, cols] = (acc[:, cols] + w0 * p0 + w1 * p1).astype(BF)

    for copy in rg_x:
        copy.wait_recv()
    sum_x = rgr[0].astype(F32) + rgr[1].astype(F32) + rgr[2].astype(F32) + rgr[3].astype(F32)
    rgy[y] = sum_x.astype(BF)
    rg_y = [cp.make(rgy.at[y], rgy.at[y], peer_y(dy)) for dy in (2, 1, 3)]
    for copy in rg_y:
        go(copy)

    for dx in (1, 3, 2):
        a1_cp[dx].wait_recv()
    sum_a = pa[0].astype(F32) + ra[1].astype(F32) + ra[2].astype(F32) + ra[3].astype(F32)
    for yy in range(4):
        pa2[yy] = sum_a[yy * T : (yy + 1) * T, :].astype(BF)
    a2_cp = {}
    for dy in (2, 1, 3):
        a2_cp[dy] = cp.make(pa2.at[(y + dy) % 4], ra2.at[dy], peer_y(dy))
        go(a2_cp[dy])
    for dy in (1, 3, 2):
        b1_cp[dy].wait_recv()
    b2_cp = {}
    for dx in (2, 1, 3, 0):
        sum_b = pb[y, dx].astype(F32)
        for dy in (1, 2, 3):
            sum_b += rb[dy, dx].astype(F32)
        pb2[dx] = sum_b.astype(BF)
        if dx != 0:
            b2_cp[dx] = cp.make(pb2.at[dx], rb2.at[dx], peer(dx, 0))
            go(b2_cp[dx])

    for copy in rg_y:
        copy.wait_recv()
    rgf[...] = rgy[0].astype(F32) + rgy[1].astype(F32) + rgy[2].astype(F32) + rgy[3].astype(F32)
    rg_out = cp.make(rgf, rgo, core_dev)
    go(rg_out)

    for dy in (1, 3, 2):
        a2_cp[dy].wait_recv()
    res_a = pa2[y].astype(F32)
    for dy in (1, 2, 3):
        res_a += ra2[dy].astype(F32)
    for dx in (1, 3, 2):
        b2_cp[dx].wait_recv()
    res_b = pb2[0].astype(F32)
    for dx in (1, 2, 3):
        res_b += rb2[dx].astype(F32)
    for h in range(2):
        fin[h, :, 0:W] = res_a[h * (T // 2) : (h + 1) * (T // 2), :]
        fin[h, :, W:H] = res_b[h * (T // 2) : (h + 1) * (T // 2), :]
    fin_cp = cp.make(fin.at[1 - c], fin_x, core_dev)
    go(fin_cp)

    @pl.when(upper)
    def _():
        hg_o[...] = own_g[...]

    @pl.when(lower)
    def _():
        for j in range(4):
            mirror_out[j].wait_recv()
            cols = slice(j * W, (j + 1) * W)
            hg_o[:, cols] = (own_g[:, cols].astype(F32) + mgr[j].astype(F32)).astype(BF)

    here = pl.ds(pl.multiple_of(c * H, H), H)
    there = pl.ds(pl.multiple_of((1 - c) * H, H), H)
    rg_out.wait_recv()
    rg_o[:, here] = rgf[0:8, :]
    rg_o[:, there] = rgo[0:8, :]
    gg_o[:, here] = rgf[8:9, :]
    gg_o[:, there] = rgo[8:9, :]
    fin_cp.wait_recv()
    sg_o[:, here] = fin[c]
    sg_o[:, there] = fin_x[...]

    for copy in started:
        if not any(copy is b_cp[o] for o in b_cp):
            copy.wait_send()

    @pl.when(lower)
    def _():
        for copy in mirror_in:
            copy.wait_send()

    @pl.when(upper)
    def _():
        mir_cp.wait_send()
        for copy in mirror_out:
            copy.wait_send()


def hand_on(*refs):
    for source, target in zip(refs[:5], refs[5:]):
        target[...] = source[...]


def per_device(
    hidden, expert_ids, cotangent, skip_weight, norm_gain, router_weight,
    gate_weight, up_weight, down_weight,
):
    T, D = hidden.shape[1:]
    FF = gate_weight.shape[-1]
    E = lax.axis_size("expert")
    CAP = min(T, 3 * T // E)
    W, H = D // 4, D // 2
    slots = E * CAP
    vmem = pl.BlockSpec(memory_space=pltpu.VMEM)
    anywhere = pl.BlockSpec(memory_space=pl.ANY)
    a2a = pltpu.VMEM((E, CAP, D), BF)
    scratch = [
        pltpu.VMEM((2 * D, D), BF), pltpu.VMEM((D, FF), BF), pltpu.VMEM((D, FF), BF), pltpu.VMEM((FF, D), BF),
        pltpu.VMEM((4, T, W), BF), pltpu.VMEM((T, D), BF), pltpu.VMEM((4, T, W), BF), pltpu.VMEM((2 * D, 2 * T), BF),
        pltpu.VMEM((T, slots), BF), pltpu.VMEM((T, slots), BF), pltpu.VMEM((slots, T), BF),
        a2a, a2a, a2a, a2a, a2a, a2a, a2a, a2a, pltpu.VMEM((E, CAP, 128), BF), pltpu.VMEM((E, CAP, 128), BF),
        pltpu.VMEM((slots, FF), F32), pltpu.VMEM((slots, FF), BF), pltpu.VMEM((slots, FF), BF), pltpu.VMEM((slots, FF), BF),
        pltpu.VMEM((T, D), F32), pltpu.VMEM((T, D), BF), pltpu.VMEM((T, D), F32),
        pltpu.VMEM((2, 16, H), BF), pltpu.VMEM((16, H), BF), pltpu.VMEM((4, 16, H), BF), pltpu.VMEM((4, 16, H), BF),
        pltpu.VMEM((16, H), F32), pltpu.VMEM((16, H), F32),
        pltpu.VMEM((2, T, H), BF), pltpu.VMEM((T, H), BF), pltpu.VMEM((2 * T, H), BF),
        pltpu.VMEM((4, T, W), BF), pltpu.VMEM((4, T, W), BF), pltpu.VMEM((T, D), BF),
        pltpu.VMEM((4, 4 * T, W), BF), pltpu.VMEM((4, 4 * T, W), BF), pltpu.VMEM((4, T, W), BF), pltpu.VMEM((4, T, W), BF),
        pltpu.VMEM((4, 4, T, W), BF), pltpu.VMEM((4, 4, T, W), BF), pltpu.VMEM((4, T, W), BF), pltpu.VMEM((4, T, W), BF),
        pltpu.VMEM((2, T // 2, H), F32), pltpu.VMEM((T // 2, H), F32),
        pltpu.SemaphoreType.DMA((4,)), pltpu.SemaphoreType.DMA((N_SEM,)), pltpu.SemaphoreType.DMA((N_SEM,)),
    ]
    results = pl.pallas_call(
        kernel,
        out_shape=(
            jax.ShapeDtypeStruct((T, D), BF),
            jax.ShapeDtypeStruct((T, D), BF),
            jax.ShapeDtypeStruct((T // 2, D), F32),
            jax.ShapeDtypeStruct((8, D), F32),
            jax.ShapeDtypeStruct((1, D), F32),
        ),
        in_specs=[vmem] * 5 + [anywhere] * 4,
        out_specs=[vmem] * 5,
        scratch_shapes=scratch,
        compiler_params=pltpu.CompilerParams(
            collective_id=0, has_side_effects=True, vmem_limit_bytes=60 * 1024 * 1024
        ),
    )(
        hidden[0], expert_ids[0].T, cotangent[0], norm_gain, router_weight[0].T,
        skip_weight[0], gate_weight[0, 0], up_weight[0, 0], down_weight[0, 0],
    )
    out, hidden_grad, skip_grad, router, gain = pl.pallas_call(
        hand_on,
        out_shape=tuple(jax.ShapeDtypeStruct(r.shape, r.dtype) for r in results),
        in_specs=[vmem] * 5,
        out_specs=[vmem] * 5,
    )(*results)
    return (out[None], hidden_grad[None], skip_grad[None], router.T[None], gain)


def solution(mesh):
    return jax.shard_map(
        per_device,
        mesh=mesh,
        in_specs=(
            P("section", ("expert", "dp"), None),
            P("section", ("expert", "dp"), None),
            P("section", ("expert", "dp"), None),
            P("section", None, None),
            P("section", None),
            P("section", None, None),
            P("section", "expert", None, None),
            P("section", "expert", None, None),
            P("section", "expert", None, None),
        ),
        out_specs=(
            P("section", ("expert", "dp"), None),
            P("section", ("expert", "dp"), None),
            P("section", ("expert", "dp"), None),
            P("section", None, None),
            P("section", None),
        ),
        check_vma=False,
    )
```

```python
import functools

import jax
import jax.numpy as jnp
from jax import lax
from jax.experimental import pallas as pl
from jax.experimental.pallas import tpu as pltpu
from jax.sharding import PartitionSpec as P

norm_eps = 1e-06
MESH = pl.DeviceIdType.MESH
BF = jnp.bfloat16
F32 = jnp.float32


def dot(left, right):
    return jnp.dot(left, right, preferred_element_type=F32)


def dot_rt(left, right):
    return lax.dot_general(left, right, (((1,), (1,)), ((), ())), preferred_element_type=F32)


def dot_lt(left, right):
    return lax.dot_general(left, right, (((0,), (0,)), ((), ())), preferred_element_type=F32)


def loop(count, body):
    for i in range(count):
        body(i)


class Copies:
    def __init__(self, send_sems, recv_sems):
        self.send_sems, self.recv_sems, self.used = send_sems, recv_sems, 0

    def make(self, src, dst, device):
        k = self.used
        self.used += 1
        return pltpu.make_async_remote_copy(
            src_ref=src,
            dst_ref=dst,
            send_sem=self.send_sems.at[k],
            recv_sem=self.recv_sems.at[k],
            device_id=device,
            device_id_type=MESH,
        )


N_SEM = 104
DISTANCES = [(0, 0), (1, 0), (3, 0), (0, 1), (2, 1), (2, 0), (1, 1), (3, 1)]
GROUPS = [(0, 5), (5, 8)]
SEND_FIRST, SEND_LAST = [4, 3, 1, 2], [6, 7, 5]
O_FIRST, O_LAST = [3, 1, 2], [4, 6, 7, 5]


def kernel(
    hid, ids, cot, gain, rw, skip_h, gate_h, up_h, down_h,
    out_o, hg_o, sg_o, rg_o, gg_o,
    skip_v, gate_v, up_v, down_v,
    mir, jto, ja, jb,
    a0, a1, sl,
    gsend, grecv, nsend, nrecv, osend, orecv, bsend, brecv, wsend, wrecv,
    ga, act, gg, gu,
    acc, normed, gn,
    rgs, r1, r2,
    gmq, ga_x, gb_x,
    mgs, mgr, own_g,
    pa, pb, ra, rb,
    local_sems, send_sems, recv_sems,
):
    T, D = hid.shape
    FF = gate_v.shape[1]
    E = 8
    CAP = nsend.shape[1]
    HALF = E // 2 * CAP
    W = D // 4
    H = D // 2
    n_sec = lax.axis_size("section")
    s = lax.axis_index("section")
    e = lax.axis_index("expert")
    d = lax.axis_index("dp")
    x, yh = e // 2, e % 2
    yl, c = d // 2, d % 2
    y = yh * 2 + yl
    upper = s >= n_sec // 2
    lower = s < n_sec // 2

    mirror_dev = (n_sec - 1 - s, e, d)
    core_dev = (s, e, d + 1 - 2 * c)

    def peer(dx, f):
        return (s, ((x + dx) % 4) * 2 + (yh + f) % 2, (d + 2 * f) % 4)

    def peer_x(dx, core):
        return (s, ((x + dx) % 4) * 2 + yh, yl * 2 + core)

    def peer_y(dy, core):
        yy = (y + dy) % 4
        return (s, x * 2 + yy // 2, (yy % 2) * 2 + core)

    cp = Copies(send_sems, recv_sems)
    started = []

    def go(copy):
        copy.start()
        started.append(copy)

    closed = []

    def sent(copy):
        copy.wait_send()
        closed.append(copy)

    loads = [
        pltpu.make_async_copy(src, dst, local_sems.at[i])
        for i, (src, dst) in enumerate(
            [(skip_h, skip_v), (down_h, down_v), (gate_h, gate_v), (up_h, up_v)]
        )
    ]
    for load in loads:
        load.start()

    barrier = pltpu.get_barrier_semaphore()
    greeted = [mirror_dev, core_dev]
    greeted += [peer(dx, f) for f in range(2) for dx in range(4) if (dx, f) != (0, 0)]
    greeted += [(s, e, (d + 2) % 4), (s, x * 2 + (yh + 1) % 2, d)]
    greeted += [peer_x(k, 1 - c) for k in (1, 2, 3)] + [peer_y(k, 1 - c) for k in (1, 2, 3)]
    for device in greeted:
        pl.semaphore_signal(barrier, inc=1, device_id=device, device_id_type=MESH)
    pl.semaphore_wait(barrier, len(greeted))

    mirror_in = [cp.make(hid.at[:, pl.ds(j * W, W)], mir.at[j], mirror_dev) for j in range(4)]

    @pl.when(lower)
    def _():
        for copy in mirror_in:
            copy.start()

    def relative(names):
        dx = ((names >> 1) - x + 4) & 3
        f = ((names & 1) - yh + 2) & 1
        label = jnp.zeros_like(names)
        for o, (dx_o, f_o) in enumerate(DISTANCES):
            label = jnp.where((dx == dx_o) & (f == f_o), o, label)
        return label

    lane = lax.broadcasted_iota(jnp.int32, (T, 128), 1)
    row = lax.broadcasted_iota(jnp.int32, (T, 128), 0)
    eye = jnp.where(lane == row, 1.0, 0.0).astype(BF)
    names = dot_rt(eye, ids[...].astype(F32).astype(BF)).astype(jnp.int32)
    id0, id1 = names[:, 0:1], names[:, 1:2]
    rel0, rel1 = relative(id0), relative(id1)
    c0, c1 = rel0 == lane, rel1 == lane
    counts = jnp.where(c0, 1.0, 0.0) + jnp.where(c1, 1.0, 0.0)
    earlier = jnp.where(lane < row, 1.0, 0.0).astype(BF)
    before = dot(earlier, counts.astype(BF))
    rank0 = jnp.sum(jnp.where(c0, before, 0.0), axis=1, keepdims=True)
    rank1 = jnp.sum(jnp.where(c1, before, 0.0), axis=1, keepdims=True)
    slots = lax.broadcasted_iota(jnp.int32, (T, E * CAP), 1).astype(F32)
    at0 = jnp.where(rel0.astype(F32) * CAP + rank0 == slots, 1.0, 0.0)
    at1 = jnp.where(rel1.astype(F32) * CAP + rank1 == slots, 1.0, 0.0)
    a0[...] = at0.astype(BF)
    a1[...] = at1.astype(BF)
    sl[...] = dot_lt((at0 + at1).astype(BF), eye).astype(BF)

    def place(rows, send, recv):
        def tile(i):
            cols = pl.ds(i * W, W)
            placed = dot(sl[...], rows[:, cols]).astype(BF)
            for o in range(E):
                block = placed[o * CAP : (o + 1) * CAP, :]
                if o == 0:
                    recv[0, :, cols] = block
                else:
                    send[o, :, cols] = block

        loop(D // W, tile)

    def dispatch(send, recv, copies, labels):
        for o in labels:
            copies[o] = cp.make(send.at[o], recv.at[o], peer(*DISTANCES[o]))
            go(copies[o])

    def give_back(send, recv, copies, labels):
        for o in labels:
            if o != 0:
                dx, f = DISTANCES[o]
                copies[o] = cp.make(send.at[o], recv.at[o], peer((4 - dx) % 4, f))
                go(copies[o])

    place(cot, gsend, grecv)
    g_cp, n_cp = {}, {}
    dispatch(gsend, grecv, g_cp, [4, 5, 6, 7, 1, 2, 3])

    mine = pl.ds(pl.multiple_of(c * T, T), T)

    def turn(rows, k):
        jto[k // 4, k % 4] = rows.T

    loop(8, lambda k: turn(hid[:, k * T : (k + 1) * T], k))
    ja_early = [cp.make(jto.at[0:2, (y + dy) % 4], ja.at[dy, 0:2, :, mine], peer_y(dy, c)) for dy in (2, 1, 3)]
    ja_late = [cp.make(jto.at[2:4, (y + dy) % 4], ja.at[dy, 2:4, :, mine], peer_y(dy, c)) for dy in (2, 1, 3)]
    jb_all = [((x + dx) % 4, cp.make(jto.at[(x + dx) % 4], jb.at[dx, :, :, mine], peer_x(dx, c))) for dx in (2, 1, 3)]
    loads[0].wait()

    def own_mix(i):
        cols = pl.ds(i * W, W)
        acc[:, cols] = dot(hid[...], skip_v[0:D, cols])

    loop(D // W, own_mix)

    @pl.when(upper)
    def _():
        for j in range(4):
            mirror_in[j].wait_recv()

            def add_mix(i, j=j):
                cols = pl.ds(i * W, W)
                acc[:, cols] += dot(mir[j], skip_v[D + j * W : D + (j + 1) * W, cols])

            loop(D // W, add_mix)

    wide = acc[...].astype(BF).astype(F32)
    acc[...] = wide
    inv_rms = lax.rsqrt(jnp.mean(wide * wide, axis=1, keepdims=True) + norm_eps)
    normed[...] = (wide * inv_rms * gain[...]).astype(BF)

    place(normed, nsend, nrecv)
    dispatch(nsend, nrecv, n_cp, SEND_FIRST)

    lane8 = lax.broadcasted_iota(jnp.int32, (T, 8), 1)
    k0, k1 = id0 == lane8, id1 == lane8
    logits = dot_rt(normed[...], rw[...])
    s0 = jax.nn.sigmoid(jnp.sum(jnp.where(k0, logits, 0.0), axis=1, keepdims=True))
    s1 = jax.nn.sigmoid(jnp.sum(jnp.where(k1, logits, 0.0), axis=1, keepdims=True))
    total = s0 + s1
    w0, w1 = s0 / total, s1 / total

    @pl.when(upper)
    def _():
        loop(8, lambda k: turn(mir[k // 2, :, k % 2 * T : (k % 2 + 1) * T], 8 + k))

    @pl.when(lower)
    def _():
        jto[2:4] = jnp.zeros((2, 4, T, T), BF)

    loads[1].wait()
    for o in g_cp:
        g_cp[o].wait_recv()

    def grad_act(i):
        cols = pl.ds(i * W, W)
        rows = grecv[...].reshape(E * CAP, D)
        ga[:, cols] = dot_rt(rows, down_v[cols, :])

    loop(FF // W, grad_act)

    loads[2].wait()
    loads[3].wait()

    for o in SEND_FIRST:
        sent(n_cp[o])
    dispatch(nsend, nrecv, n_cp, SEND_LAST)

    def split(values, send, recv, cols, labels):
        for k, o in enumerate(labels):
            block = values[k * CAP : (k + 1) * CAP, :]
            if o == 0:
                recv[0, :, cols] = block
            else:
                send[o, :, cols] = block

    o_cp, b_cp, w_cp = {}, {}, {}

    def group(first, last):
        labels = range(first, last)
        count = (last - first) * CAP
        rows = slice(first * CAP, last * CAP)
        for o in labels:
            if o != 0:
                n_cp[o].wait_recv()
        for i in range(FF // W):
            cols = slice(i * W, (i + 1) * W)
            frames = nrecv[first:last].reshape(count, D)
            pre_gate = dot(frames, gate_v[:, cols])
            pre_up = dot(frames, up_v[:, cols])
            grad = ga[rows, cols]
            sig = jax.nn.sigmoid(pre_gate)
            silu = pre_gate * sig
            act[rows, cols] = (silu * pre_up).astype(BF)
            gg[rows, cols] = (grad * pre_up * sig * (1.0 + pre_gate * (1.0 - sig))).astype(BF)
            gu[rows, cols] = (grad * silu).astype(BF)
        if first == 0:
            for copy in ja_early:
                go(copy)
            for xx, copy in jb_all:
                started.append(copy)

                @pl.when(xx < 2)
                def _(copy=copy):
                    copy.start()

        for i in range(D // W):
            cols = slice(i * W, (i + 1) * W)
            grads = dot_rt(gg[rows, :], gate_v[cols, :]) + dot_rt(gu[rows, :], up_v[cols, :])
            split(grads.astype(BF), bsend, brecv, cols, labels)
        give_back(bsend, brecv, b_cp, labels)
        along = 0.0
        for i in range(D // W):
            cols = slice(i * W, (i + 1) * W)
            values = dot(act[rows, :], down_v[:, cols]).astype(BF)
            split(values, osend, orecv, cols, labels)
            grads = grecv[first:last, :, cols].reshape(count, W).astype(F32)
            along += jnp.sum(values.astype(F32) * grads, axis=1, keepdims=True)
        high = along.astype(BF)
        low = (along - high.astype(F32)).astype(BF)
        half = lax.broadcasted_iota(jnp.int32, (count, 128), 1) < 64
        split(jnp.where(half, high, low), wsend, wrecv, slice(0, 128), labels)
        give_back(wsend, wrecv, w_cp, labels)

    for first, last in GROUPS:
        group(first, last)
    for o in b_cp:
        sent(b_cp[o])
    for copy in ja_late:
        go(copy)
    for xx, copy in jb_all:

        @pl.when(xx >= 2)
        def _(copy=copy):
            copy.start()

    give_back(osend, orecv, o_cp, O_FIRST)

    for o in w_cp:
        w_cp[o].wait_recv()
    rows_w = wrecv[...].reshape(E * CAP, 128)
    t0, t1 = dot(a0[...], rows_w), dot(a1[...], rows_w)
    grad_w0 = t0[:, 0:1] + t0[:, 64:65]
    grad_w1 = t1[:, 0:1] + t1[:, 64:65]
    weighted = w0 * grad_w0 + w1 * grad_w1
    gl0 = (grad_w0 - weighted) / total * s0 * (1.0 - s0)
    gl1 = (grad_w1 - weighted) / total * s1 * (1.0 - s1)
    grad_logits = (jnp.where(k0, gl0, 0.0) + jnp.where(k1, gl1, 0.0)).astype(BF)

    for o in b_cp:
        b_cp[o].wait_recv()
    mean_term = 0.0
    for i in range(D // W):
        cols = slice(i * W, (i + 1) * W)
        rows_b = brecv[:, :, cols].reshape(E * CAP, W)
        grad_normed = w0 * dot(a0[...], rows_b) + w1 * dot(a1[...], rows_b)
        grad_normed += dot(grad_logits, rw[:, cols])
        unit = acc[:, cols] * inv_rms
        gain_term = jnp.sum(grad_normed * unit, axis=0, keepdims=True)
        router_term = dot_lt(grad_logits, normed[:, cols])
        both = jnp.concatenate([router_term, jnp.broadcast_to(gain_term, (8, W))], axis=0)
        rgs[i // 2, :, (i % 2) * W : (i % 2 + 1) * W] = both.astype(BF)
        grad_unit = grad_normed * gain[:, cols]
        gn[:, cols] = grad_unit
        mean_term += jnp.sum(grad_unit * unit, axis=1, keepdims=True)
    mean_term = mean_term / D
    rg_1 = [cp.make(rgs.at[1 - c], r1.at[y, c], core_dev)]
    rg_1 += [cp.make(rgs.at[cc], r1.at[y, c], peer_y(dy, cc)) for dy in (2, 1, 3) for cc in (c, 1 - c)]
    for copy in rg_1:
        go(copy)
    r1[y, c] = rgs[c]
    for i in range(D // W):
        cols = slice(i * W, (i + 1) * W)
        unit = acc[:, cols] * inv_rms
        grad_mixed = cot[:, cols].astype(F32) + inv_rms * (gn[:, cols] - unit * mean_term)
        gmq[i] = grad_mixed.astype(BF)
    gm = jnp.concatenate([gmq[0], gmq[1], gmq[2], gmq[3]], axis=1)

    mirror_out = [cp.make(mgs.at[j], mgr.at[j], mirror_dev) for j in range(4)]

    def send_mirror(j):
        mgs[j] = dot_rt(gm, skip_v[D + j * W : D + (j + 1) * W, :]).astype(BF)
        mirror_out[j].start()

    @pl.when(upper)
    def _():
        send_mirror(0)

    gm_a = {0: [cp.make(gmq.at[2 * (1 - c)], ga_x.at[0, mine], core_dev)]}
    gm_b = {0: [cp.make(gmq.at[2 * (1 - c) + 1], gb_x.at[0, mine], core_dev)]}
    for k in (2, 1, 3):
        gm_a[k] = [cp.make(gmq.at[2 * cc], ga_x.at[k, mine], peer_y(k, cc)) for cc in (c, 1 - c)]
        gm_b[k] = [cp.make(gmq.at[2 * cc + 1], gb_x.at[k, mine], peer_x(k, cc)) for cc in (c, 1 - c)]
    for k in (2, 1, 3, 0):
        for copy in gm_a[k] + gm_b[k]:
            go(copy)
    ga_x[0, mine] = gmq[2 * c]
    gb_x[0, mine] = gmq[2 * c + 1]

    @pl.when(upper)
    def _():
        for j in (1, 2, 3):
            send_mirror(j)

    for copy in rg_1:
        copy.wait_recv()
    sum_y = 0.0
    for yy in range(4):
        for cc in range(2):
            sum_y += r1[yy, cc].astype(F32)
    r2[c, x] = sum_y.astype(BF)
    rg_2 = [cp.make(r2.at[c, x], r2.at[c, x], core_dev)]
    rg_2 += [cp.make(r2.at[c, x], r2.at[c, x], peer_x(dx, cc)) for dx in (2, 1, 3) for cc in (c, 1 - c)]
    for copy in rg_2:
        go(copy)

    def own_grad(j):
        cols = pl.ds(j * W, W)
        own_g[:, cols] = dot_rt(gm, skip_v[cols, :]).astype(BF)

    loop(4, own_grad)

    for xx in range(4):
        ja[0, xx, :, mine] = jto[xx, y]
    jb[0, :, :, mine] = jto[x]
    for copy in ja_early + ja_late + [copy for _, copy in jb_all]:
        copy.wait_recv()
    j_core = [cp.make(j.at[:, :, :, mine], j.at[:, :, :, mine], core_dev) for j in (ja, jb)]
    for copy in j_core:
        go(copy)

    for k in range(4):
        for copy in gm_a[k] + gm_b[k]:
            sent(copy)
    give_back(osend, orecv, o_cp, O_LAST)
    for copy in j_core:
        copy.wait_recv()

    def product(frames, grads, copies, parts):
        total = 0.0
        for k in (0, 1, 3, 2):
            for copy in copies[k]:
                copy.wait_recv()
            total += dot(frames[k].reshape(4 * T, 2 * T), grads[k])
        for k in range(4):
            parts[k] = total[k * T : (k + 1) * T, :].astype(BF)

    def pass_on(parts, sums, at, peer_of):
        half = [pl.ds(pl.multiple_of(cc * (T // 2), T // 2), T // 2) for cc in (c, 1 - c)]
        copies = []
        for k in (2, 1, 3):
            for cc, rows in zip((c, 1 - c), half):
                copies.append(cp.make(parts.at[(at + k) % 4, rows], sums.at[c, k], peer_of(k, cc)))
        copies.append(cp.make(parts.at[at, half[1]], sums.at[c, 0], core_dev))
        for copy in copies:
            go(copy)
        sums[c, 0] = parts[at, half[0]]
        return copies

    product(ja, ga_x, gm_a, pa)
    ra_cp = pass_on(pa, ra, x, peer_x)
    product(jb, gb_x, gm_b, pb)
    rb_cp = pass_on(pb, rb, y, peer_y)

    for o in o_cp:
        o_cp[o].wait_recv()
    for i in range(D // W):
        cols = slice(i * W, (i + 1) * W)
        rows_o = orecv[:, :, cols].reshape(E * CAP, W)
        p0, p1 = dot(a0[...], rows_o), dot(a1[...], rows_o)
        out_o[:, cols] = (acc[:, cols] + w0 * p0 + w1 * p1).astype(BF)

    for copy in rg_2:
        copy.wait_recv()
    for h in range(2):
        cols = slice(h * H, (h + 1) * H)
        sums = 0.0
        for xx in range(4):
            sums += r2[h, xx].astype(F32)
        rg_o[:, cols] = sums[0:8, :]
        gg_o[:, cols] = sums[8:9, :]

    for copy in ra_cp + rb_cp:
        copy.wait_recv()
    for cc in range(2):
        for part, start in ((ra, cc * H), (rb, cc * H + W)):
            sums = 0.0
            for k in range(4):
                sums += part[cc, k].astype(F32)
            sg_o[:, start : start + W] = sums

    @pl.when(upper)
    def _():
        hg_o[...] = own_g[...]

    @pl.when(lower)
    def _():
        for j in range(4):
            mirror_out[j].wait_recv()
            cols = slice(j * W, (j + 1) * W)
            hg_o[:, cols] = (own_g[:, cols].astype(F32) + mgr[j].astype(F32)).astype(BF)

    for copy in started:
        if not any(copy is other for other in closed):
            copy.wait_send()

    @pl.when(lower)
    def _():
        for copy in mirror_in:
            copy.wait_send()

    @pl.when(upper)
    def _():
        for copy in mirror_out:
            copy.wait_send()


def hand_on(*refs):
    for source, target in zip(refs[:5], refs[5:]):
        target[...] = source[...]


def per_device(
    hidden, expert_ids, cotangent, skip_weight, norm_gain, router_weight,
    gate_weight, up_weight, down_weight,
):
    T, D = hidden.shape[1:]
    FF = gate_weight.shape[-1]
    E = lax.axis_size("expert")
    CAP = min(T, 3 * T // E)
    W, H = D // 4, D // 2
    slots = E * CAP
    vmem = pl.BlockSpec(memory_space=pltpu.VMEM)
    anywhere = pl.BlockSpec(memory_space=pl.ANY)
    a2a = pltpu.VMEM((E, CAP, D), BF)
    scratch = [
        pltpu.VMEM((2 * D, D), BF), pltpu.VMEM((D, FF), BF), pltpu.VMEM((D, FF), BF), pltpu.VMEM((FF, D), BF),
        pltpu.VMEM((4, T, W), BF), pltpu.VMEM((4, 4, T, T), BF), pltpu.VMEM((4, 4, T, 2 * T), BF), pltpu.VMEM((4, 4, T, 2 * T), BF),
        pltpu.VMEM((T, slots), BF), pltpu.VMEM((T, slots), BF), pltpu.VMEM((slots, T), BF),
        a2a, a2a, a2a, a2a, a2a, a2a, a2a, a2a, pltpu.VMEM((E, CAP, 128), BF), pltpu.VMEM((E, CAP, 128), BF),
        pltpu.VMEM((slots, FF), F32), pltpu.VMEM((slots, FF), BF), pltpu.VMEM((slots, FF), BF), pltpu.VMEM((slots, FF), BF),
        pltpu.VMEM((T, D), F32), pltpu.VMEM((T, D), BF), pltpu.VMEM((T, D), F32),
        pltpu.VMEM((2, 16, H), BF), pltpu.VMEM((4, 2, 16, H), BF), pltpu.VMEM((2, 4, 16, H), BF),
        pltpu.VMEM((4, T, W), BF), pltpu.VMEM((4, 2 * T, W), BF), pltpu.VMEM((4, 2 * T, W), BF),
        pltpu.VMEM((4, T, W), BF), pltpu.VMEM((4, T, W), BF), pltpu.VMEM((T, D), BF),
        pltpu.VMEM((4, T, W), BF), pltpu.VMEM((4, T, W), BF), pltpu.VMEM((2, 4, T // 2, W), BF), pltpu.VMEM((2, 4, T // 2, W), BF),
        pltpu.SemaphoreType.DMA((4,)), pltpu.SemaphoreType.DMA((N_SEM,)), pltpu.SemaphoreType.DMA((N_SEM,)),
    ]
    results = pl.pallas_call(
        kernel,
        out_shape=(
            jax.ShapeDtypeStruct((T, D), BF),
            jax.ShapeDtypeStruct((T, D), BF),
            jax.ShapeDtypeStruct((T // 2, D), F32),
            jax.ShapeDtypeStruct((8, D), F32),
            jax.ShapeDtypeStruct((1, D), F32),
        ),
        in_specs=[vmem] * 5 + [anywhere] * 4,
        out_specs=[vmem] * 5,
        scratch_shapes=scratch,
        compiler_params=pltpu.CompilerParams(
            collective_id=0, has_side_effects=True, vmem_limit_bytes=60 * 1024 * 1024
        ),
    )(
        hidden[0], expert_ids[0].T, cotangent[0], norm_gain, router_weight[0].T,
        skip_weight[0], gate_weight[0, 0], up_weight[0, 0], down_weight[0, 0],
    )
    out, hidden_grad, skip_grad, router, gain = pl.pallas_call(
        hand_on,
        out_shape=tuple(jax.ShapeDtypeStruct(r.shape, r.dtype) for r in results),
        in_specs=[vmem] * 5,
        out_specs=[vmem] * 5,
    )(*results)
    return (out[None], hidden_grad[None], skip_grad[None], router.T[None], gain)


def solution(mesh):
    return jax.shard_map(
        per_device,
        mesh=mesh,
        in_specs=(
            P("section", ("expert", "dp"), None),
            P("section", ("expert", "dp"), None),
            P("section", ("expert", "dp"), None),
            P("section", None, None),
            P("section", None),
            P("section", None, None),
            P("section", "expert", None, None),
            P("section", "expert", None, None),
            P("section", "expert", None, None),
        ),
        out_specs=(
            P("section", ("expert", "dp"), None),
            P("section", ("expert", "dp"), None),
            P("section", ("expert", "dp"), None),
            P("section", None, None),
            P("section", None),
        ),
        check_vma=False,
    )
```

```python
import functools

import jax
import jax.numpy as jnp
from jax import lax
from jax.experimental import pallas as pl
from jax.experimental.pallas import tpu as pltpu
from jax.sharding import PartitionSpec as P

norm_eps = 1e-06
MESH = pl.DeviceIdType.MESH
BF = jnp.bfloat16
F32 = jnp.float32


def dot(left, right):
    return jnp.dot(left, right, preferred_element_type=F32)


def dot_rt(left, right):
    return lax.dot_general(left, right, (((1,), (1,)), ((), ())), preferred_element_type=F32)


def dot_lt(left, right):
    return lax.dot_general(left, right, (((0,), (0,)), ((), ())), preferred_element_type=F32)


def loop(count, body):
    for i in range(count):
        body(i)


class Copies:
    def __init__(self, send_sems, recv_sems):
        self.send_sems, self.recv_sems, self.used = send_sems, recv_sems, 0

    def make(self, src, dst, device):
        k = self.used
        self.used += 1
        return pltpu.make_async_remote_copy(
            src_ref=src,
            dst_ref=dst,
            send_sem=self.send_sems.at[k],
            recv_sem=self.recv_sems.at[k],
            device_id=device,
            device_id_type=MESH,
        )


N_SEM = 104
DISTANCES = [(0, 0), (1, 0), (3, 0), (0, 1), (2, 1), (2, 0), (1, 1), (3, 1)]
GROUPS = [(0, 5), (5, 8)]
SEND_FIRST, SEND_LAST = [4, 3, 1, 2], [6, 7, 5]
O_FIRST, O_LAST = [4, 6, 5], [7, 3, 1, 2]


def kernel(
    hid, ids, cot, gain, rw, skip_h, gate_h, up_h, down_h,
    out_o, hg_o, sg_o, rg_o, gg_o,
    skip_v, gate_v, up_v, down_v,
    mir, jto, ja, jb,
    a0, a1, sl,
    gsend, grecv, nsend, nrecv, osend, orecv, bsend, brecv, wsend, wrecv,
    ga, act, gg, gu,
    acc, normed, gn,
    rgs, r1, r2,
    gmq, ga_x, gb_x,
    mgs, mgr, own_g,
    pa, pb, ra, rb,
    local_sems, send_sems, recv_sems,
):
    T, D = hid.shape
    FF = gate_v.shape[1]
    E = 8
    CAP = nsend.shape[1]
    HALF = E // 2 * CAP
    W = D // 4
    H = D // 2
    n_sec = lax.axis_size("section")
    s = lax.axis_index("section")
    e = lax.axis_index("expert")
    d = lax.axis_index("dp")
    x, yh = e // 2, e % 2
    yl, c = d // 2, d % 2
    y = yh * 2 + yl
    upper = s >= n_sec // 2
    lower = s < n_sec // 2

    mirror_dev = (n_sec - 1 - s, e, d)
    core_dev = (s, e, d + 1 - 2 * c)

    def peer(dx, f):
        return (s, ((x + dx) % 4) * 2 + (yh + f) % 2, (d + 2 * f) % 4)

    def peer_x(dx, core):
        return (s, ((x + dx) % 4) * 2 + yh, yl * 2 + core)

    def peer_y(dy, core):
        yy = (y + dy) % 4
        return (s, x * 2 + yy // 2, (yy % 2) * 2 + core)

    cp = Copies(send_sems, recv_sems)
    started = []

    def go(copy):
        copy.start()
        started.append(copy)

    closed = []

    def sent(copy):
        copy.wait_send()
        closed.append(copy)

    loads = [
        pltpu.make_async_copy(src, dst, local_sems.at[i])
        for i, (src, dst) in enumerate(
            [(skip_h, skip_v), (down_h, down_v), (gate_h, gate_v), (up_h, up_v)]
        )
    ]
    for load in loads:
        load.start()

    barrier = pltpu.get_barrier_semaphore()
    greeted = [mirror_dev, core_dev]
    greeted += [peer(dx, f) for f in range(2) for dx in range(4) if (dx, f) != (0, 0)]
    greeted += [(s, e, (d + 2) % 4), (s, x * 2 + (yh + 1) % 2, d)]
    greeted += [peer_x(k, 1 - c) for k in (1, 2, 3)] + [peer_y(k, 1 - c) for k in (1, 2, 3)]
    for device in greeted:
        pl.semaphore_signal(barrier, inc=1, device_id=device, device_id_type=MESH)

    def relative(names):
        dx = ((names >> 1) - x + 4) & 3
        f = ((names & 1) - yh + 2) & 1
        label = jnp.zeros_like(names)
        for o, (dx_o, f_o) in enumerate(DISTANCES):
            label = jnp.where((dx == dx_o) & (f == f_o), o, label)
        return label

    lane = lax.broadcasted_iota(jnp.int32, (T, 128), 1)
    row = lax.broadcasted_iota(jnp.int32, (T, 128), 0)
    eye = jnp.where(lane == row, 1.0, 0.0).astype(BF)
    names = dot_rt(eye, ids[...].astype(F32).astype(BF)).astype(jnp.int32)
    id0, id1 = names[:, 0:1], names[:, 1:2]
    rel0, rel1 = relative(id0), relative(id1)
    c0, c1 = rel0 == lane, rel1 == lane
    counts = jnp.where(c0, 1.0, 0.0) + jnp.where(c1, 1.0, 0.0)
    earlier = jnp.where(lane < row, 1.0, 0.0).astype(BF)
    before = dot(earlier, counts.astype(BF))
    rank0 = jnp.sum(jnp.where(c0, before, 0.0), axis=1, keepdims=True)
    rank1 = jnp.sum(jnp.where(c1, before, 0.0), axis=1, keepdims=True)
    slots = lax.broadcasted_iota(jnp.int32, (T, E * CAP), 1).astype(F32)
    at0 = jnp.where(rel0.astype(F32) * CAP + rank0 == slots, 1.0, 0.0)
    at1 = jnp.where(rel1.astype(F32) * CAP + rank1 == slots, 1.0, 0.0)
    a0[...] = at0.astype(BF)
    a1[...] = at1.astype(BF)
    sl[...] = dot_lt((at0 + at1).astype(BF), eye).astype(BF)

    def place(rows, send, recv):
        def tile(i):
            cols = pl.ds(i * W, W)
            placed = dot(sl[...], rows[:, cols]).astype(BF)
            for o in range(E):
                block = placed[o * CAP : (o + 1) * CAP, :]
                if o == 0:
                    recv[0, :, cols] = block
                else:
                    send[o, :, cols] = block

        loop(D // W, tile)

    def dispatch(send, recv, copies, labels):
        for o in labels:
            copies[o] = cp.make(send.at[o], recv.at[o], peer(*DISTANCES[o]))
            go(copies[o])

    def give_back(send, recv, copies, labels):
        for o in labels:
            if o != 0:
                dx, f = DISTANCES[o]
                copies[o] = cp.make(send.at[o], recv.at[o], peer((4 - dx) % 4, f))
                go(copies[o])

    place(cot, gsend, grecv)
    pl.semaphore_wait(barrier, len(greeted))

    mirror_in = [cp.make(hid.at[:, pl.ds(j * W, W)], mir.at[j], mirror_dev) for j in range(4)]

    @pl.when(lower)
    def _():
        for copy in mirror_in:
            copy.start()

    g_cp, n_cp = {}, {}
    dispatch(gsend, grecv, g_cp, [4, 5, 6, 7, 1, 2, 3])

    mine = pl.ds(pl.multiple_of(c * T, T), T)

    def turn(rows, k):
        jto[k // 4, k % 4] = rows.T

    loop(8, lambda k: turn(hid[:, k * T : (k + 1) * T], k))
    ja_early = [cp.make(jto.at[0:2, (y + dy) % 4], ja.at[dy, 0:2, :, mine], peer_y(dy, c)) for dy in (2, 1, 3)]
    ja_late = [cp.make(jto.at[2:4, (y + dy) % 4], ja.at[dy, 2:4, :, mine], peer_y(dy, c)) for dy in (2, 1, 3)]
    jb_all = [((x + dx) % 4, cp.make(jto.at[(x + dx) % 4], jb.at[dx, :, :, mine], peer_x(dx, c))) for dx in (2, 1, 3)]
    loads[0].wait()

    def own_mix(i):
        cols = pl.ds(i * W, W)
        acc[:, cols] = dot(hid[...], skip_v[0:D, cols])

    loop(D // W, own_mix)

    @pl.when(upper)
    def _():
        for j in range(4):
            mirror_in[j].wait_recv()

            def add_mix(i, j=j):
                cols = pl.ds(i * W, W)
                acc[:, cols] += dot(mir[j], skip_v[D + j * W : D + (j + 1) * W, cols])

            loop(D // W, add_mix)

    wide = acc[...].astype(BF).astype(F32)
    acc[...] = wide
    inv_rms = lax.rsqrt(jnp.mean(wide * wide, axis=1, keepdims=True) + norm_eps)
    normed[...] = (wide * inv_rms * gain[...]).astype(BF)

    place(normed, nsend, nrecv)
    dispatch(nsend, nrecv, n_cp, SEND_FIRST)

    lane8 = lax.broadcasted_iota(jnp.int32, (T, 8), 1)
    k0, k1 = id0 == lane8, id1 == lane8
    logits = dot_rt(normed[...], rw[...])
    s0 = jax.nn.sigmoid(jnp.sum(jnp.where(k0, logits, 0.0), axis=1, keepdims=True))
    s1 = jax.nn.sigmoid(jnp.sum(jnp.where(k1, logits, 0.0), axis=1, keepdims=True))
    total = s0 + s1
    w0, w1 = s0 / total, s1 / total

    @pl.when(upper)
    def _():
        loop(8, lambda k: turn(mir[k // 2, :, k % 2 * T : (k % 2 + 1) * T], 8 + k))

    @pl.when(lower)
    def _():
        jto[2:4] = jnp.zeros((2, 4, T, T), BF)

    loads[1].wait()
    for o in g_cp:
        g_cp[o].wait_recv()

    def grad_act(i):
        cols = pl.ds(i * W, W)
        rows = grecv[...].reshape(E * CAP, D)
        ga[:, cols] = dot_rt(rows, down_v[cols, :])

    loop(FF // W, grad_act)

    loads[2].wait()
    loads[3].wait()

    for o in SEND_FIRST:
        sent(n_cp[o])
    dispatch(nsend, nrecv, n_cp, SEND_LAST)
    for copy in ja_early:
        go(copy)

    def split(values, send, recv, cols, labels):
        for k, o in enumerate(labels):
            block = values[k * CAP : (k + 1) * CAP, :]
            if o == 0:
                recv[0, :, cols] = block
            else:
                send[o, :, cols] = block

    o_cp, b_cp, w_cp = {}, {}, {}

    def group(first, last):
        labels = range(first, last)
        count = (last - first) * CAP
        rows = slice(first * CAP, last * CAP)
        for o in labels:
            if o != 0:
                n_cp[o].wait_recv()
        for i in range(FF // W):
            cols = slice(i * W, (i + 1) * W)
            frames = nrecv[first:last].reshape(count, D)
            pre_gate = dot(frames, gate_v[:, cols])
            pre_up = dot(frames, up_v[:, cols])
            grad = ga[rows, cols]
            sig = jax.nn.sigmoid(pre_gate)
            silu = pre_gate * sig
            act[rows, cols] = (silu * pre_up).astype(BF)
            gg[rows, cols] = (grad * pre_up * sig * (1.0 + pre_gate * (1.0 - sig))).astype(BF)
            gu[rows, cols] = (grad * silu).astype(BF)
        for i in range(D // W):
            cols = slice(i * W, (i + 1) * W)
            grads = dot_rt(gg[rows, :], gate_v[cols, :]) + dot_rt(gu[rows, :], up_v[cols, :])
            split(grads.astype(BF), bsend, brecv, cols, labels)
        give_back(bsend, brecv, b_cp, labels)
    def group_outputs(first, last):
        labels = range(first, last)
        count = (last - first) * CAP
        rows = slice(first * CAP, last * CAP)
        along = 0.0
        for i in range(D // W):
            cols = slice(i * W, (i + 1) * W)
            values = dot(act[rows, :], down_v[:, cols]).astype(BF)
            split(values, osend, orecv, cols, labels)
            grads = grecv[first:last, :, cols].reshape(count, W).astype(F32)
            along += jnp.sum(values.astype(F32) * grads, axis=1, keepdims=True)
        high = along.astype(BF)
        low = (along - high.astype(F32)).astype(BF)
        half = lax.broadcasted_iota(jnp.int32, (count, 128), 1) < 64
        split(jnp.where(half, high, low), wsend, wrecv, slice(0, 128), labels)
        give_back(wsend, wrecv, w_cp, labels)

    for first, last in GROUPS:
        group(first, last)
    for first, last in GROUPS:
        group_outputs(first, last)
    for o in b_cp:
        sent(b_cp[o])
    for copy in ja_late + [copy for _, copy in jb_all]:
        go(copy)

    for o in w_cp:
        w_cp[o].wait_recv()
    rows_w = wrecv[...].reshape(E * CAP, 128)
    t0, t1 = dot(a0[...], rows_w), dot(a1[...], rows_w)
    grad_w0 = t0[:, 0:1] + t0[:, 64:65]
    grad_w1 = t1[:, 0:1] + t1[:, 64:65]
    weighted = w0 * grad_w0 + w1 * grad_w1
    gl0 = (grad_w0 - weighted) / total * s0 * (1.0 - s0)
    gl1 = (grad_w1 - weighted) / total * s1 * (1.0 - s1)
    grad_logits = (jnp.where(k0, gl0, 0.0) + jnp.where(k1, gl1, 0.0)).astype(BF)

    for o in b_cp:
        b_cp[o].wait_recv()
    mean_term = 0.0
    for i in range(D // W):
        cols = slice(i * W, (i + 1) * W)
        rows_b = brecv[:, :, cols].reshape(E * CAP, W)
        grad_normed = w0 * dot(a0[...], rows_b) + w1 * dot(a1[...], rows_b)
        grad_normed += dot(grad_logits, rw[:, cols])
        unit = acc[:, cols] * inv_rms
        gain_term = jnp.sum(grad_normed * unit, axis=0, keepdims=True)
        router_term = dot_lt(grad_logits, normed[:, cols])
        both = jnp.concatenate([router_term, jnp.broadcast_to(gain_term, (8, W))], axis=0)
        rgs[i // 2, :, (i % 2) * W : (i % 2 + 1) * W] = both.astype(BF)
        grad_unit = grad_normed * gain[:, cols]
        gn[:, cols] = grad_unit
        mean_term += jnp.sum(grad_unit * unit, axis=1, keepdims=True)
    mean_term = mean_term / D
    rg_1 = [cp.make(rgs.at[1 - c], r1.at[y, c], core_dev)]
    rg_1 += [cp.make(rgs.at[cc], r1.at[y, c], peer_y(dy, cc)) for dy in (2, 1, 3) for cc in (c, 1 - c)]
    for copy in rg_1:
        go(copy)
    r1[y, c] = rgs[c]
    for i in range(D // W):
        cols = slice(i * W, (i + 1) * W)
        unit = acc[:, cols] * inv_rms
        grad_mixed = cot[:, cols].astype(F32) + inv_rms * (gn[:, cols] - unit * mean_term)
        gmq[i] = grad_mixed.astype(BF)
    gm = jnp.concatenate([gmq[0], gmq[1], gmq[2], gmq[3]], axis=1)

    mirror_out = [cp.make(mgs.at[j], mgr.at[j], mirror_dev) for j in range(4)]

    def send_mirror(j):
        mgs[j] = dot_rt(gm, skip_v[D + j * W : D + (j + 1) * W, :]).astype(BF)
        mirror_out[j].start()

    @pl.when(upper)
    def _():
        send_mirror(0)

    gm_a = {0: [cp.make(gmq.at[2 * (1 - c)], ga_x.at[0, mine], core_dev)]}
    gm_b = {0: [cp.make(gmq.at[2 * (1 - c) + 1], gb_x.at[0, mine], core_dev)]}
    for k in (2, 1, 3):
        gm_a[k] = [cp.make(gmq.at[2 * cc], ga_x.at[k, mine], peer_y(k, cc)) for cc in (c, 1 - c)]
        gm_b[k] = [cp.make(gmq.at[2 * cc + 1], gb_x.at[k, mine], peer_x(k, cc)) for cc in (c, 1 - c)]
    for k in (2, 1, 3, 0):
        for copy in gm_a[k] + gm_b[k]:
            go(copy)
    ga_x[0, mine] = gmq[2 * c]
    gb_x[0, mine] = gmq[2 * c + 1]

    @pl.when(upper)
    def _():
        for j in (1, 2, 3):
            send_mirror(j)

    give_back(osend, orecv, o_cp, O_FIRST)

    for copy in rg_1:
        copy.wait_recv()
    sum_y = 0.0
    for yy in range(4):
        for cc in range(2):
            sum_y += r1[yy, cc].astype(F32)
    r2[c, x] = sum_y.astype(BF)
    rg_2 = [cp.make(r2.at[c, x], r2.at[c, x], core_dev)]
    rg_2 += [cp.make(r2.at[c, x], r2.at[c, x], peer_x(dx, cc)) for dx in (2, 1, 3) for cc in (c, 1 - c)]
    for copy in rg_2:
        go(copy)

    def own_grad(j):
        cols = pl.ds(j * W, W)
        own_g[:, cols] = dot_rt(gm, skip_v[cols, :]).astype(BF)

    loop(4, own_grad)

    for xx in range(4):
        ja[0, xx, :, mine] = jto[xx, y]
    jb[0, :, :, mine] = jto[x]
    for copy in ja_early + ja_late + [copy for _, copy in jb_all]:
        copy.wait_recv()
    j_core = [cp.make(j.at[:, :, :, mine], j.at[:, :, :, mine], core_dev) for j in (ja, jb)]
    for copy in j_core:
        go(copy)

    give_back(osend, orecv, o_cp, O_LAST)
    for copy in j_core:
        copy.wait_recv()

    def product(frames, grads, copies, parts):
        total = 0.0
        for k in (0, 1, 3, 2):
            for copy in copies[k]:
                copy.wait_recv()
            total += dot(frames[k].reshape(4 * T, 2 * T), grads[k])
        for k in range(4):
            parts[k] = total[k * T : (k + 1) * T, :].astype(BF)

    def pass_on(parts, sums, at, peer_of):
        half = [pl.ds(pl.multiple_of(cc * (T // 2), T // 2), T // 2) for cc in (c, 1 - c)]
        copies = []
        for k in (2, 1, 3):
            for cc, rows in zip((c, 1 - c), half):
                copies.append(cp.make(parts.at[(at + k) % 4, rows], sums.at[c, k], peer_of(k, cc)))
        copies.append(cp.make(parts.at[at, half[1]], sums.at[c, 0], core_dev))
        for copy in copies:
            go(copy)
        sums[c, 0] = parts[at, half[0]]
        return copies

    product(ja, ga_x, gm_a, pa)
    ra_cp = pass_on(pa, ra, x, peer_x)
    product(jb, gb_x, gm_b, pb)
    rb_cp = pass_on(pb, rb, y, peer_y)

    for o in o_cp:
        o_cp[o].wait_recv()
    for i in range(D // W):
        cols = slice(i * W, (i + 1) * W)
        rows_o = orecv[:, :, cols].reshape(E * CAP, W)
        p0, p1 = dot(a0[...], rows_o), dot(a1[...], rows_o)
        out_o[:, cols] = (acc[:, cols] + w0 * p0 + w1 * p1).astype(BF)

    for copy in rg_2:
        copy.wait_recv()
    for h in range(2):
        cols = slice(h * H, (h + 1) * H)
        sums = 0.0
        for xx in range(4):
            sums += r2[h, xx].astype(F32)
        rg_o[:, cols] = sums[0:8, :]
        gg_o[:, cols] = sums[8:9, :]

    for copy in ra_cp + rb_cp:
        copy.wait_recv()
    for cc in range(2):
        for part, start in ((ra, cc * H), (rb, cc * H + W)):
            sums = 0.0
            for k in range(4):
                sums += part[cc, k].astype(F32)
            sg_o[:, start : start + W] = sums

    @pl.when(upper)
    def _():
        hg_o[...] = own_g[...]

    @pl.when(lower)
    def _():
        for j in range(4):
            mirror_out[j].wait_recv()
            cols = slice(j * W, (j + 1) * W)
            hg_o[:, cols] = (own_g[:, cols].astype(F32) + mgr[j].astype(F32)).astype(BF)

    for copy in started:
        if not any(copy is other for other in closed):
            copy.wait_send()

    @pl.when(lower)
    def _():
        for copy in mirror_in:
            copy.wait_send()

    @pl.when(upper)
    def _():
        for copy in mirror_out:
            copy.wait_send()


def hand_on(*refs):
    for source, target in zip(refs[:5], refs[5:]):
        target[...] = source[...]


def per_device(
    hidden, expert_ids, cotangent, skip_weight, norm_gain, router_weight,
    gate_weight, up_weight, down_weight,
):
    T, D = hidden.shape[1:]
    FF = gate_weight.shape[-1]
    E = lax.axis_size("expert")
    CAP = min(T, 3 * T // E)
    W, H = D // 4, D // 2
    slots = E * CAP
    vmem = pl.BlockSpec(memory_space=pltpu.VMEM)
    anywhere = pl.BlockSpec(memory_space=pl.ANY)
    a2a = pltpu.VMEM((E, CAP, D), BF)
    scratch = [
        pltpu.VMEM((2 * D, D), BF), pltpu.VMEM((D, FF), BF), pltpu.VMEM((D, FF), BF), pltpu.VMEM((FF, D), BF),
        pltpu.VMEM((4, T, W), BF), pltpu.VMEM((4, 4, T, T), BF), pltpu.VMEM((4, 4, T, 2 * T), BF), pltpu.VMEM((4, 4, T, 2 * T), BF),
        pltpu.VMEM((T, slots), BF), pltpu.VMEM((T, slots), BF), pltpu.VMEM((slots, T), BF),
        a2a, a2a, a2a, a2a, a2a, a2a, a2a, a2a, pltpu.VMEM((E, CAP, 128), BF), pltpu.VMEM((E, CAP, 128), BF),
        pltpu.VMEM((slots, FF), F32), pltpu.VMEM((slots, FF), BF), pltpu.VMEM((slots, FF), BF), pltpu.VMEM((slots, FF), BF),
        pltpu.VMEM((T, D), F32), pltpu.VMEM((T, D), BF), pltpu.VMEM((T, D), F32),
        pltpu.VMEM((2, 16, H), BF), pltpu.VMEM((4, 2, 16, H), BF), pltpu.VMEM((2, 4, 16, H), BF),
        pltpu.VMEM((4, T, W), BF), pltpu.VMEM((4, 2 * T, W), BF), pltpu.VMEM((4, 2 * T, W), BF),
        pltpu.VMEM((4, T, W), BF), pltpu.VMEM((4, T, W), BF), pltpu.VMEM((T, D), BF),
        pltpu.VMEM((4, T, W), BF), pltpu.VMEM((4, T, W), BF), pltpu.VMEM((2, 4, T // 2, W), BF), pltpu.VMEM((2, 4, T // 2, W), BF),
        pltpu.SemaphoreType.DMA((4,)), pltpu.SemaphoreType.DMA((N_SEM,)), pltpu.SemaphoreType.DMA((N_SEM,)),
    ]
    results = pl.pallas_call(
        kernel,
        out_shape=(
            jax.ShapeDtypeStruct((T, D), BF),
            jax.ShapeDtypeStruct((T, D), BF),
            jax.ShapeDtypeStruct((T // 2, D), F32),
            jax.ShapeDtypeStruct((8, D), F32),
            jax.ShapeDtypeStruct((1, D), F32),
        ),
        in_specs=[vmem] * 5 + [anywhere] * 4,
        out_specs=[vmem] * 5,
        scratch_shapes=scratch,
        compiler_params=pltpu.CompilerParams(
            collective_id=0, has_side_effects=True, vmem_limit_bytes=60 * 1024 * 1024
        ),
    )(
        hidden[0], expert_ids[0].T, cotangent[0], norm_gain, router_weight[0].T,
        skip_weight[0], gate_weight[0, 0], up_weight[0, 0], down_weight[0, 0],
    )
    out, hidden_grad, skip_grad, router, gain = pl.pallas_call(
        hand_on,
        out_shape=tuple(jax.ShapeDtypeStruct(r.shape, r.dtype) for r in results),
        in_specs=[vmem] * 5,
        out_specs=[vmem] * 5,
    )(*results)
    return (out[None], hidden_grad[None], skip_grad[None], router.T[None], gain)


def solution(mesh):
    return jax.shard_map(
        per_device,
        mesh=mesh,
        in_specs=(
            P("section", ("expert", "dp"), None),
            P("section", ("expert", "dp"), None),
            P("section", ("expert", "dp"), None),
            P("section", None, None),
            P("section", None),
            P("section", None, None),
            P("section", "expert", None, None),
            P("section", "expert", None, None),
            P("section", "expert", None, None),
        ),
        out_specs=(
            P("section", ("expert", "dp"), None),
            P("section", ("expert", "dp"), None),
            P("section", ("expert", "dp"), None),
            P("section", None, None),
            P("section", None),
        ),
        check_vma=False,
    )
```

```python
import functools

import jax
import jax.numpy as jnp
from jax import lax
from jax.experimental import pallas as pl
from jax.experimental.pallas import tpu as pltpu
from jax.sharding import PartitionSpec as P

norm_eps = 1e-06
MESH = pl.DeviceIdType.MESH
BF = jnp.bfloat16
F32 = jnp.float32


def dot(left, right):
    return jnp.dot(left, right, preferred_element_type=F32)


def dot_rt(left, right):
    return lax.dot_general(left, right, (((1,), (1,)), ((), ())), preferred_element_type=F32)


def dot_lt(left, right):
    return lax.dot_general(left, right, (((0,), (0,)), ((), ())), preferred_element_type=F32)


def loop(count, body):
    for i in range(count):
        body(i)


class Copies:
    def __init__(self, send_sems, recv_sems):
        self.send_sems, self.recv_sems, self.used = send_sems, recv_sems, 0

    def make(self, src, dst, device):
        k = self.used
        self.used += 1
        return pltpu.make_async_remote_copy(
            src_ref=src,
            dst_ref=dst,
            send_sem=self.send_sems.at[k],
            recv_sem=self.recv_sems.at[k],
            device_id=device,
            device_id_type=MESH,
        )


N_SEM = 104
DISTANCES = [(0, 0), (1, 0), (3, 0), (0, 1), (2, 1), (2, 0), (1, 1), (3, 1)]
GROUPS = [(0, 5), (5, 8)]
SEND_FIRST, SEND_LAST = [4, 3, 1, 2], [6, 7, 5]
O_FIRST, O_LAST = [4, 6, 5], [7, 3, 1, 2]


def kernel(
    hid, ids, cot, gain, rw, skip_h, gate_h, up_h, down_h,
    out_o, hg_o, sg_o, rg_o, gg_o,
    skip_v, gate_v, up_v, down_v,
    mir, jto, ja, jb,
    a0, a1, sl,
    gsend, grecv, nsend, nrecv, osend, orecv, bsend, brecv, wsend, wrecv,
    ga, act, gg, gu,
    acc, normed, gn,
    rgs, r1, r2,
    gmq, ga_x, gb_x,
    mgs, mgr, own_g,
    pa, pb, ra, rb,
    local_sems, send_sems, recv_sems,
):
    T, D = hid.shape
    FF = gate_v.shape[1]
    E = 8
    CAP = nsend.shape[1]
    HALF = E // 2 * CAP
    W = D // 4
    H = D // 2
    n_sec = lax.axis_size("section")
    s = lax.axis_index("section")
    e = lax.axis_index("expert")
    d = lax.axis_index("dp")
    x, yh = e // 2, e % 2
    yl, c = d // 2, d % 2
    y = yh * 2 + yl
    upper = s >= n_sec // 2
    lower = s < n_sec // 2

    mirror_dev = (n_sec - 1 - s, e, d)
    core_dev = (s, e, d + 1 - 2 * c)

    def peer(dx, f):
        return (s, ((x + dx) % 4) * 2 + (yh + f) % 2, (d + 2 * f) % 4)

    def peer_x(dx, core):
        return (s, ((x + dx) % 4) * 2 + yh, yl * 2 + core)

    def peer_y(dy, core):
        yy = (y + dy) % 4
        return (s, x * 2 + yy // 2, (yy % 2) * 2 + core)

    cp = Copies(send_sems, recv_sems)
    started = []

    def go(copy):
        copy.start()
        started.append(copy)

    closed = []

    def sent(copy):
        copy.wait_send()
        closed.append(copy)

    loads = [
        pltpu.make_async_copy(src, dst, local_sems.at[i])
        for i, (src, dst) in enumerate(
            [(skip_h, skip_v), (down_h, down_v), (gate_h, gate_v), (up_h, up_v)]
        )
    ]
    for load in loads:
        load.start()

    barrier = pltpu.get_barrier_semaphore()
    greeted = [mirror_dev, core_dev]
    greeted += [peer(dx, f) for f in range(2) for dx in range(4) if (dx, f) != (0, 0)]
    greeted += [(s, e, (d + 2) % 4), (s, x * 2 + (yh + 1) % 2, d)]
    greeted += [peer_x(k, 1 - c) for k in (1, 2, 3)] + [peer_y(k, 1 - c) for k in (1, 2, 3)]
    for device in greeted:
        pl.semaphore_signal(barrier, inc=1, device_id=device, device_id_type=MESH)

    def relative(names):
        dx = ((names >> 1) - x + 4) & 3
        f = ((names & 1) - yh + 2) & 1
        label = jnp.zeros_like(names)
        for o, (dx_o, f_o) in enumerate(DISTANCES):
            label = jnp.where((dx == dx_o) & (f == f_o), o, label)
        return label

    lane = lax.broadcasted_iota(jnp.int32, (T, 128), 1)
    row = lax.broadcasted_iota(jnp.int32, (T, 128), 0)
    eye = jnp.where(lane == row, 1.0, 0.0).astype(BF)
    names = dot_rt(eye, ids[...].astype(F32).astype(BF)).astype(jnp.int32)
    id0, id1 = names[:, 0:1], names[:, 1:2]
    rel0, rel1 = relative(id0), relative(id1)
    c0, c1 = rel0 == lane, rel1 == lane
    counts = jnp.where(c0, 1.0, 0.0) + jnp.where(c1, 1.0, 0.0)
    earlier = jnp.where(lane < row, 1.0, 0.0).astype(BF)
    before = dot(earlier, counts.astype(BF))
    rank0 = jnp.sum(jnp.where(c0, before, 0.0), axis=1, keepdims=True)
    rank1 = jnp.sum(jnp.where(c1, before, 0.0), axis=1, keepdims=True)
    slots = lax.broadcasted_iota(jnp.int32, (T, E * CAP), 1).astype(F32)
    at0 = jnp.where(rel0.astype(F32) * CAP + rank0 == slots, 1.0, 0.0)
    at1 = jnp.where(rel1.astype(F32) * CAP + rank1 == slots, 1.0, 0.0)
    a0[...] = at0.astype(BF)
    a1[...] = at1.astype(BF)
    sl[...] = dot_lt((at0 + at1).astype(BF), eye).astype(BF)

    def place(rows, send, recv):
        def tile(i):
            cols = pl.ds(i * W, W)
            placed = dot(sl[...], rows[:, cols]).astype(BF)
            for o in range(E):
                block = placed[o * CAP : (o + 1) * CAP, :]
                if o == 0:
                    recv[0, :, cols] = block
                else:
                    send[o, :, cols] = block

        loop(D // W, tile)

    def dispatch(send, recv, copies, labels):
        for o in labels:
            copies[o] = cp.make(send.at[o], recv.at[o], peer(*DISTANCES[o]))
            go(copies[o])

    def give_back(send, recv, copies, labels):
        for o in labels:
            if o != 0:
                dx, f = DISTANCES[o]
                copies[o] = cp.make(send.at[o], recv.at[o], peer((4 - dx) % 4, f))
                go(copies[o])

    place(cot, gsend, grecv)
    pl.semaphore_wait(barrier, len(greeted))

    mirror_in = [cp.make(hid.at[:, pl.ds(j * W, W)], mir.at[j], mirror_dev) for j in range(4)]

    @pl.when(lower)
    def _():
        for copy in mirror_in:
            copy.start()

    g_cp, n_cp = {}, {}
    dispatch(gsend, grecv, g_cp, [4, 5, 6, 7, 1, 2, 3])

    mine = pl.ds(pl.multiple_of(c * T, T), T)

    def turn(rows, k):
        jto[k // 4, k % 4] = rows.T

    loop(8, lambda k: turn(hid[:, k * T : (k + 1) * T], k))
    ja_early = [cp.make(jto.at[0:2, (y + dy) % 4], ja.at[dy, 0:2, :, mine], peer_y(dy, c)) for dy in (2, 1, 3)]
    ja_late = [cp.make(jto.at[2:4, (y + dy) % 4], ja.at[dy, 2:4, :, mine], peer_y(dy, c)) for dy in (2, 1, 3)]
    jb_all = [((x + dx) % 4, cp.make(jto.at[(x + dx) % 4], jb.at[dx, :, :, mine], peer_x(dx, c))) for dx in (2, 1, 3)]
    loads[0].wait()

    def own_mix(i):
        cols = pl.ds(i * W, W)
        acc[:, cols] = dot(hid[...], skip_v[0:D, cols])

    loop(D // W, own_mix)

    @pl.when(upper)
    def _():
        for j in range(4):
            mirror_in[j].wait_recv()

            def add_mix(i, j=j):
                cols = pl.ds(i * W, W)
                acc[:, cols] += dot(mir[j], skip_v[D + j * W : D + (j + 1) * W, cols])

            loop(D // W, add_mix)

    wide = acc[...].astype(BF).astype(F32)
    acc[...] = wide
    inv_rms = lax.rsqrt(jnp.mean(wide * wide, axis=1, keepdims=True) + norm_eps)
    normed[...] = (wide * inv_rms * gain[...]).astype(BF)

    place(normed, nsend, nrecv)
    dispatch(nsend, nrecv, n_cp, SEND_FIRST)

    lane8 = lax.broadcasted_iota(jnp.int32, (T, 8), 1)
    k0, k1 = id0 == lane8, id1 == lane8
    logits = dot_rt(normed[...], rw[...])
    s0 = jax.nn.sigmoid(jnp.sum(jnp.where(k0, logits, 0.0), axis=1, keepdims=True))
    s1 = jax.nn.sigmoid(jnp.sum(jnp.where(k1, logits, 0.0), axis=1, keepdims=True))
    total = s0 + s1
    w0, w1 = s0 / total, s1 / total

    @pl.when(upper)
    def _():
        loop(8, lambda k: turn(mir[k // 2, :, k % 2 * T : (k % 2 + 1) * T], 8 + k))

    @pl.when(lower)
    def _():
        jto[2:4] = jnp.zeros((2, 4, T, T), BF)

    loads[1].wait()
    for o in g_cp:
        g_cp[o].wait_recv()

    def grad_act(i):
        cols = pl.ds(i * W, W)
        rows = grecv[...].reshape(E * CAP, D)
        ga[:, cols] = dot_rt(rows, down_v[cols, :])

    loop(FF // W, grad_act)

    loads[2].wait()
    loads[3].wait()

    for o in SEND_FIRST:
        sent(n_cp[o])
    dispatch(nsend, nrecv, n_cp, SEND_LAST)

    def split(values, send, recv, cols, labels):
        for k, o in enumerate(labels):
            block = values[k * CAP : (k + 1) * CAP, :]
            if o == 0:
                recv[0, :, cols] = block
            else:
                send[o, :, cols] = block

    o_cp, b_cp, w_cp = {}, {}, {}

    def group(first, last):
        labels = range(first, last)
        count = (last - first) * CAP
        rows = slice(first * CAP, last * CAP)
        for o in labels:
            if o != 0:
                n_cp[o].wait_recv()
        for i in range(FF // W):
            cols = slice(i * W, (i + 1) * W)
            frames = nrecv[first:last].reshape(count, D)
            pre_gate = dot(frames, gate_v[:, cols])
            pre_up = dot(frames, up_v[:, cols])
            grad = ga[rows, cols]
            sig = jax.nn.sigmoid(pre_gate)
            silu = pre_gate * sig
            act[rows, cols] = (silu * pre_up).astype(BF)
            gg[rows, cols] = (grad * pre_up * sig * (1.0 + pre_gate * (1.0 - sig))).astype(BF)
            gu[rows, cols] = (grad * silu).astype(BF)
        for i in range(D // W):
            cols = slice(i * W, (i + 1) * W)
            grads = dot_rt(gg[rows, :], gate_v[cols, :]) + dot_rt(gu[rows, :], up_v[cols, :])
            split(grads.astype(BF), bsend, brecv, cols, labels)
        give_back(bsend, brecv, b_cp, labels)
    def group_outputs(first, last):
        labels = range(first, last)
        count = (last - first) * CAP
        rows = slice(first * CAP, last * CAP)
        along = 0.0
        for i in range(D // W):
            cols = slice(i * W, (i + 1) * W)
            values = dot(act[rows, :], down_v[:, cols]).astype(BF)
            split(values, osend, orecv, cols, labels)
            grads = grecv[first:last, :, cols].reshape(count, W).astype(F32)
            along += jnp.sum(values.astype(F32) * grads, axis=1, keepdims=True)
        high = along.astype(BF)
        low = (along - high.astype(F32)).astype(BF)
        half = lax.broadcasted_iota(jnp.int32, (count, 128), 1) < 64
        split(jnp.where(half, high, low), wsend, wrecv, slice(0, 128), labels)
        give_back(wsend, wrecv, w_cp, labels)

    for first, last in GROUPS:
        group(first, last)
    for first, last in GROUPS:
        group_outputs(first, last)
    for o in b_cp:
        sent(b_cp[o])
    for copy in ja_early + ja_late + [copy for _, copy in jb_all]:
        go(copy)

    for o in w_cp:
        w_cp[o].wait_recv()
    rows_w = wrecv[...].reshape(E * CAP, 128)
    t0, t1 = dot(a0[...], rows_w), dot(a1[...], rows_w)
    grad_w0 = t0[:, 0:1] + t0[:, 64:65]
    grad_w1 = t1[:, 0:1] + t1[:, 64:65]
    weighted = w0 * grad_w0 + w1 * grad_w1
    gl0 = (grad_w0 - weighted) / total * s0 * (1.0 - s0)
    gl1 = (grad_w1 - weighted) / total * s1 * (1.0 - s1)
    grad_logits = (jnp.where(k0, gl0, 0.0) + jnp.where(k1, gl1, 0.0)).astype(BF)

    for o in b_cp:
        b_cp[o].wait_recv()
    mean_term = 0.0
    for i in range(D // W):
        cols = slice(i * W, (i + 1) * W)
        rows_b = brecv[:, :, cols].reshape(E * CAP, W)
        grad_normed = w0 * dot(a0[...], rows_b) + w1 * dot(a1[...], rows_b)
        grad_normed += dot(grad_logits, rw[:, cols])
        unit = acc[:, cols] * inv_rms
        gain_term = jnp.sum(grad_normed * unit, axis=0, keepdims=True)
        router_term = dot_lt(grad_logits, normed[:, cols])
        both = jnp.concatenate([router_term, jnp.broadcast_to(gain_term, (8, W))], axis=0)
        rgs[i // 2, :, (i % 2) * W : (i % 2 + 1) * W] = both.astype(BF)
        grad_unit = grad_normed * gain[:, cols]
        gn[:, cols] = grad_unit
        mean_term += jnp.sum(grad_unit * unit, axis=1, keepdims=True)
    mean_term = mean_term / D
    rg_1 = [cp.make(rgs.at[1 - c], r1.at[y, c], core_dev)]
    rg_1 += [cp.make(rgs.at[cc], r1.at[y, c], peer_y(dy, cc)) for dy in (2, 1, 3) for cc in (c, 1 - c)]
    for copy in rg_1:
        go(copy)
    r1[y, c] = rgs[c]
    for i in range(D // W):
        cols = slice(i * W, (i + 1) * W)
        unit = acc[:, cols] * inv_rms
        grad_mixed = cot[:, cols].astype(F32) + inv_rms * (gn[:, cols] - unit * mean_term)
        gmq[i] = grad_mixed.astype(BF)
    gm = jnp.concatenate([gmq[0], gmq[1], gmq[2], gmq[3]], axis=1)

    mirror_out = [cp.make(mgs.at[j], mgr.at[j], mirror_dev) for j in range(4)]

    def send_mirror(j):
        mgs[j] = dot_rt(gm, skip_v[D + j * W : D + (j + 1) * W, :]).astype(BF)
        mirror_out[j].start()

    @pl.when(upper)
    def _():
        send_mirror(0)

    gm_a = {0: [cp.make(gmq.at[2 * (1 - c)], ga_x.at[0, mine], core_dev)]}
    gm_b = {0: [cp.make(gmq.at[2 * (1 - c) + 1], gb_x.at[0, mine], core_dev)]}
    for k in (2, 1, 3):
        gm_a[k] = [cp.make(gmq.at[2 * cc], ga_x.at[k, mine], peer_y(k, cc)) for cc in (c, 1 - c)]
        gm_b[k] = [cp.make(gmq.at[2 * cc + 1], gb_x.at[k, mine], peer_x(k, cc)) for cc in (c, 1 - c)]
    for k in (2, 1, 3, 0):
        for copy in gm_a[k] + gm_b[k]:
            go(copy)
    ga_x[0, mine] = gmq[2 * c]
    gb_x[0, mine] = gmq[2 * c + 1]

    @pl.when(upper)
    def _():
        for j in (1, 2, 3):
            send_mirror(j)

    give_back(osend, orecv, o_cp, O_FIRST)

    for copy in rg_1:
        copy.wait_recv()
    sum_y = 0.0
    for yy in range(4):
        for cc in range(2):
            sum_y += r1[yy, cc].astype(F32)
    r2[c, x] = sum_y.astype(BF)
    rg_2 = [cp.make(r2.at[c, x], r2.at[c, x], core_dev)]
    rg_2 += [cp.make(r2.at[c, x], r2.at[c, x], peer_x(dx, cc)) for dx in (2, 1, 3) for cc in (c, 1 - c)]
    for copy in rg_2:
        go(copy)

    def own_grad(j):
        cols = pl.ds(j * W, W)
        own_g[:, cols] = dot_rt(gm, skip_v[cols, :]).astype(BF)

    loop(4, own_grad)

    for xx in range(4):
        ja[0, xx, :, mine] = jto[xx, y]
    jb[0, :, :, mine] = jto[x]
    for copy in ja_early + ja_late + [copy for _, copy in jb_all]:
        copy.wait_recv()
    j_core = [cp.make(j.at[:, :, :, mine], j.at[:, :, :, mine], core_dev) for j in (ja, jb)]
    for copy in j_core:
        go(copy)

    give_back(osend, orecv, o_cp, O_LAST)
    for copy in j_core:
        copy.wait_recv()

    def product(frames, grads, copies, parts):
        total = 0.0
        for k in (0, 1, 3, 2):
            for copy in copies[k]:
                copy.wait_recv()
            total += dot(frames[k].reshape(4 * T, 2 * T), grads[k])
        for k in range(4):
            parts[k] = total[k * T : (k + 1) * T, :].astype(BF)

    def pass_on(parts, sums, at, peer_of):
        half = [pl.ds(pl.multiple_of(cc * (T // 2), T // 2), T // 2) for cc in (c, 1 - c)]
        copies = []
        for k in (2, 1, 3):
            for cc, rows in zip((c, 1 - c), half):
                copies.append(cp.make(parts.at[(at + k) % 4, rows], sums.at[c, k], peer_of(k, cc)))
        copies.append(cp.make(parts.at[at, half[1]], sums.at[c, 0], core_dev))
        for copy in copies:
            go(copy)
        sums[c, 0] = parts[at, half[0]]
        return copies

    product(ja, ga_x, gm_a, pa)
    ra_cp = pass_on(pa, ra, x, peer_x)
    product(jb, gb_x, gm_b, pb)
    rb_cp = pass_on(pb, rb, y, peer_y)

    for o in o_cp:
        o_cp[o].wait_recv()
    for i in range(D // W):
        cols = slice(i * W, (i + 1) * W)
        rows_o = orecv[:, :, cols].reshape(E * CAP, W)
        p0, p1 = dot(a0[...], rows_o), dot(a1[...], rows_o)
        out_o[:, cols] = (acc[:, cols] + w0 * p0 + w1 * p1).astype(BF)

    for copy in rg_2:
        copy.wait_recv()
    for h in range(2):
        cols = slice(h * H, (h + 1) * H)
        sums = 0.0
        for xx in range(4):
            sums += r2[h, xx].astype(F32)
        rg_o[:, cols] = sums[0:8, :]
        gg_o[:, cols] = sums[8:9, :]

    for copy in ra_cp + rb_cp:
        copy.wait_recv()
    for cc in range(2):
        for part, start in ((ra, cc * H), (rb, cc * H + W)):
            sums = 0.0
            for k in range(4):
                sums += part[cc, k].astype(F32)
            sg_o[:, start : start + W] = sums

    @pl.when(upper)
    def _():
        hg_o[...] = own_g[...]

    @pl.when(lower)
    def _():
        for j in range(4):
            mirror_out[j].wait_recv()
            cols = slice(j * W, (j + 1) * W)
            hg_o[:, cols] = (own_g[:, cols].astype(F32) + mgr[j].astype(F32)).astype(BF)

    for copy in started:
        if not any(copy is other for other in closed):
            copy.wait_send()

    @pl.when(lower)
    def _():
        for copy in mirror_in:
            copy.wait_send()

    @pl.when(upper)
    def _():
        for copy in mirror_out:
            copy.wait_send()


def hand_on(*refs):
    for source, target in zip(refs[:5], refs[5:]):
        target[...] = source[...]


def per_device(
    hidden, expert_ids, cotangent, skip_weight, norm_gain, router_weight,
    gate_weight, up_weight, down_weight,
):
    T, D = hidden.shape[1:]
    FF = gate_weight.shape[-1]
    E = lax.axis_size("expert")
    CAP = min(T, 3 * T // E)
    W, H = D // 4, D // 2
    slots = E * CAP
    vmem = pl.BlockSpec(memory_space=pltpu.VMEM)
    anywhere = pl.BlockSpec(memory_space=pl.ANY)
    a2a = pltpu.VMEM((E, CAP, D), BF)
    scratch = [
        pltpu.VMEM((2 * D, D), BF), pltpu.VMEM((D, FF), BF), pltpu.VMEM((D, FF), BF), pltpu.VMEM((FF, D), BF),
        pltpu.VMEM((4, T, W), BF), pltpu.VMEM((4, 4, T, T), BF), pltpu.VMEM((4, 4, T, 2 * T), BF), pltpu.VMEM((4, 4, T, 2 * T), BF),
        pltpu.VMEM((T, slots), BF), pltpu.VMEM((T, slots), BF), pltpu.VMEM((slots, T), BF),
        a2a, a2a, a2a, a2a, a2a, a2a, a2a, a2a, pltpu.VMEM((E, CAP, 128), BF), pltpu.VMEM((E, CAP, 128), BF),
        pltpu.VMEM((slots, FF), F32), pltpu.VMEM((slots, FF), BF), pltpu.VMEM((slots, FF), BF), pltpu.VMEM((slots, FF), BF),
        pltpu.VMEM((T, D), F32), pltpu.VMEM((T, D), BF), pltpu.VMEM((T, D), F32),
        pltpu.VMEM((2, 16, H), BF), pltpu.VMEM((4, 2, 16, H), BF), pltpu.VMEM((2, 4, 16, H), BF),
        pltpu.VMEM((4, T, W), BF), pltpu.VMEM((4, 2 * T, W), BF), pltpu.VMEM((4, 2 * T, W), BF),
        pltpu.VMEM((4, T, W), BF), pltpu.VMEM((4, T, W), BF), pltpu.VMEM((T, D), BF),
        pltpu.VMEM((4, T, W), BF), pltpu.VMEM((4, T, W), BF), pltpu.VMEM((2, 4, T // 2, W), BF), pltpu.VMEM((2, 4, T // 2, W), BF),
        pltpu.SemaphoreType.DMA((4,)), pltpu.SemaphoreType.DMA((N_SEM,)), pltpu.SemaphoreType.DMA((N_SEM,)),
    ]
    results = pl.pallas_call(
        kernel,
        out_shape=(
            jax.ShapeDtypeStruct((T, D), BF),
            jax.ShapeDtypeStruct((T, D), BF),
            jax.ShapeDtypeStruct((T // 2, D), F32),
            jax.ShapeDtypeStruct((8, D), F32),
            jax.ShapeDtypeStruct((1, D), F32),
        ),
        in_specs=[vmem] * 5 + [anywhere] * 4,
        out_specs=[vmem] * 5,
        scratch_shapes=scratch,
        compiler_params=pltpu.CompilerParams(
            collective_id=0, has_side_effects=True, vmem_limit_bytes=60 * 1024 * 1024
        ),
    )(
        hidden[0], expert_ids[0].T, cotangent[0], norm_gain, router_weight[0].T,
        skip_weight[0], gate_weight[0, 0], up_weight[0, 0], down_weight[0, 0],
    )
    out, hidden_grad, skip_grad, router, gain = pl.pallas_call(
        hand_on,
        out_shape=tuple(jax.ShapeDtypeStruct(r.shape, r.dtype) for r in results),
        in_specs=[vmem] * 5,
        out_specs=[vmem] * 5,
    )(*results)
    return (out[None], hidden_grad[None], skip_grad[None], router.T[None], gain)


def solution(mesh):
    return jax.shard_map(
        per_device,
        mesh=mesh,
        in_specs=(
            P("section", ("expert", "dp"), None),
            P("section", ("expert", "dp"), None),
            P("section", ("expert", "dp"), None),
            P("section", None, None),
            P("section", None),
            P("section", None, None),
            P("section", "expert", None, None),
            P("section", "expert", None, None),
            P("section", "expert", None, None),
        ),
        out_specs=(
            P("section", ("expert", "dp"), None),
            P("section", ("expert", "dp"), None),
            P("section", ("expert", "dp"), None),
            P("section", None, None),
            P("section", None),
        ),
        check_vma=False,
    )
```
